256 devices in a mesh: dp: 16 (over x, z_lo, core), hid: 16 (over y, z_hi).
Axes of the slice: x: 4, y: 4, z: 8 (z_hi: 4, z_lo: 2; z = z_hi * 2 + z_lo), core: 2. Of those that a mesh axis runs over, the one named last changes fastest.
Arguments:
- tokens: bfloat16 [6144, 4096], P(('dp', 'hid')), may hold values from -6 to 6
- cotangent: bfloat16 [6144, 4096], P(('dp', 'hid')), may hold values from -6 to 6
- w_in: bfloat16 [16, 128, 128, 128], P(None, 'hid'), may hold values from -0.1875 to 0.1875
- w_out: bfloat16 [16, 128, 128, 128], P(None, 'hid'), may hold values from -0.09375 to 0.09375
- block_index: int32 [16, 128], P(None, 'hid'), may hold values from 0 to 31, as said below
- live_count: int32 [128], P('hid'), may hold values from 2 to 16, as said below
Outputs:
- mixed: bfloat16 [6144, 4096], P(('dp', 'hid'))
- token_grad: bfloat16 [6144, 4096], P(('dp', 'hid'))
- in_grad: float32 [16, 128, 128, 128], P('dp', 'hid')
- out_grad: float32 [16, 128, 128, 128], P('dp', 'hid')
The draws below stay inside these ranges and needn't reach their ends.
Inputs may be any that keep to these rules, and one draw needn't show every extreme that they name: For k < live_count[c] the numbers block_index[k, c] of one hidden block c are distinct; the other entries are not read. `live_count`: some hidden block has all 16 slots live.
All inputs are finite; a program needn't handle non-finite values.
Results may differ from the reference program's by a relative error of at most 0.02.
Values may be sent and summed in bfloat16 or wider, within the bound.
A program may use at most 128 MiB of HBM per device.

```python
import math
import jax
import jax.numpy as jnp
from jax import lax

MODEL_WIDTH = 4096
F = 16384
BLK = 128
K = 16
TOK_DEV = 384
DB = 32
FB = 128
FB_DEV = 8
TOKENS = 6144
N_DP = 16
N_HID = 16


def shuffle_column(column_key):
    return jax.random.permutation(column_key, DB)


def draw_block_index(key, part):
    key = jax.random.fold_in(key, 11)
    column_keys = jax.random.split(key, FB)
    orders = jax.vmap(shuffle_column)(column_keys)
    return orders[:, :K].T.astype(jnp.int32)


def draw_live_count(key, part):
    key = jax.random.fold_in(key, 23)
    level_key, count_key, full_key = jax.random.split(key, 3)
    levels = jax.random.randint(level_key, (FB // FB_DEV,), 0, 3)
    ceiling = jnp.repeat(K // jnp.power(2, levels), FB_DEV)
    counts = jax.random.randint(count_key, (FB,), ceiling // 2, ceiling + 1)
    chosen = jax.random.randint(full_key, (), 0, FB)
    counts = jnp.where(jnp.arange(FB) == chosen, K, counts)
    return counts.astype(jnp.int32)


def block_levels(own_key, dims, cuts, smallest, top_value):
    def one(dim, blocks):
        steps = jax.random.uniform(jax.random.fold_in(jax.random.fold_in(own_key, 6), dim), (blocks,), jnp.float32, smallest / len(cuts), top_value / len(cuts))
        return jnp.repeat(jnp.exp(steps), dims[dim] // blocks).reshape((-1,) + (1,) * (len(dims) - dim - 1))

    factor_of = one(*cuts[0])
    for cut in cuts[1:]:
        factor_of = factor_of * one(*cut)
    return factor_of


def centred(key, extent, deviation, reach, pieces=(), dtype=jnp.bfloat16):
    factor_of = block_levels(key, extent, pieces, -0.22, 0.18) if pieces else 1.0
    entries = jax.random.normal(key, extent, jnp.float32) * deviation * factor_of
    return jnp.minimum(jnp.maximum(entries, -reach), reach).astype(dtype)


def setup_inputs(seed: int = 0) -> dict:
    keys = jax.random.split(jax.random.key(seed), 7)
    tokens = centred(keys[0], (TOKENS, MODEL_WIDTH), 1.0, 6.0, ((0, 256),))
    cotangent = centred(keys[1], (TOKENS, MODEL_WIDTH), 1.0, 6.0, ((0, 256),))
    w_in = centred(keys[2], (K, FB, BLK, BLK), (MODEL_WIDTH // 4) ** -0.5, 0.1875, ((1, 16),))
    w_out = centred(keys[3], (K, FB, BLK, BLK), (F // 4) ** -0.5, 0.09375, ((1, 16),))
    block_index = draw_block_index(jax.random.fold_in(keys[6], 71), 0)
    live_count = draw_live_count(jax.random.fold_in(keys[6], 71), 0)
    return {"tokens": tokens, "cotangent": cotangent, "w_in": w_in, "w_out": w_out, "block_index": block_index, "live_count": live_count}


gelu_root = 0.7978845608028654
gelu_cubic = 0.044715

def gelu_parts(pre):
    argument = gelu_root * (pre + gelu_cubic * pre * pre * pre)
    tangent = jnp.tanh(argument)
    activated = 0.5 * pre * (1.0 + tangent)
    slope = 0.5 * (1.0 + tangent) + 0.5 * pre * (1.0 - tangent * tangent) * gelu_root * (1.0 + 3.0 * gelu_cubic * pre * pre)
    return (activated, slope)

def shard_terms(rows_in, rows_back, weight_in, weight_out, slot_rows, live_slots, grad_scale):
    grouped_token_rows = rows_in.shape[0]
    active = jnp.arange(K)[:, None] < live_slots[None, :]
    target = jnp.where(active, slot_rows, DB).astype(jnp.int32)
    selection_mask = (target[:, :, None] == jnp.arange(DB).astype(jnp.int32)[None, None, :]).astype(jnp.float32)
    blocks_in = rows_in.astype(jnp.float32).reshape(grouped_token_rows, DB, BLK)
    blocks_back = rows_back.astype(jnp.float32).reshape(grouped_token_rows, DB, BLK)
    picked = jnp.take(blocks_in, target, axis=1, mode='fill', fill_value=0.0)
    picked_back = jnp.take(blocks_back, target, axis=1, mode='fill', fill_value=0.0)
    weight_in32 = weight_in.astype(jnp.float32)
    weight_out32 = weight_out.astype(jnp.float32)
    pre = jnp.einsum('tkci,kcin->tcn', picked, weight_in32)
    activated, slope = gelu_parts(pre)
    hidden = activated.astype(jnp.bfloat16).astype(jnp.float32)
    spread_tokens = jnp.einsum('tcn,kcnm->tkcm', hidden, weight_out32)
    output_portion = jnp.einsum('yhop,hon->ynp', spread_tokens, selection_mask).reshape(grouped_token_rows, MODEL_WIDTH).astype(jnp.bfloat16)
    hidden_grad = jnp.einsum('tkcm,kcnm->tcn', picked_back, weight_out32)
    pre_grad = (hidden_grad * slope).astype(jnp.bfloat16).astype(jnp.float32)
    spread_back = jnp.einsum('tcn,kcin->tkci', pre_grad, weight_in32)
    token_part = jnp.einsum('tkci,kcb->tbi', spread_back, selection_mask).reshape(grouped_token_rows, MODEL_WIDTH).astype(jnp.bfloat16)
    in_part = (jnp.einsum('tkci,tcn->kcin', picked, pre_grad) * grad_scale).astype(jnp.bfloat16)
    output_weight_portion = (jnp.einsum('tcn,tkcm->kcnm', hidden, picked_back) * grad_scale).astype(jnp.bfloat16)
    return (output_portion, token_part, in_part, output_weight_portion)

def reference(tokens, cotangent, w_in, w_out, block_index, live_count):
    grad_scale = 1.0 / math.sqrt(TOKENS)
    shard_in = w_in.reshape(K, N_HID, FB_DEV, BLK, BLK).transpose(1, 0, 2, 3, 4)
    shard_out = w_out.reshape(K, N_HID, FB_DEV, BLK, BLK).transpose(1, 0, 2, 3, 4)
    shard_index = block_index.reshape(K, N_HID, FB_DEV).transpose(1, 0, 2)
    shard_count = live_count.reshape(N_HID, FB_DEV)
    group_in = tokens.reshape(N_DP, TOK_DEV, MODEL_WIDTH)
    group_back = cotangent.reshape(N_DP, TOK_DEV, MODEL_WIDTH)

    def group_step(totals, group_input_rows):
        rows_in, rows_back = group_input_rows

        def shard_step(running, shard_data):
            weight_in, weight_out, slot_rows, live_slots = shard_data
            output_portion, token_part, in_part, output_weight_portion = shard_terms(rows_in, rows_back, weight_in, weight_out, slot_rows, live_slots, grad_scale)
            return ((running[0] + output_portion.astype(jnp.float32), running[1] + token_part.astype(jnp.float32)), (in_part, output_weight_portion))
        empty_sum = jnp.zeros((TOK_DEV, MODEL_WIDTH), jnp.float32)
        (out_sum, token_sum), (in_parts, outw_parts) = lax.scan(shard_step, (empty_sum, empty_sum), (shard_in, shard_out, shard_index, shard_count))
        in_full = in_parts.transpose(1, 0, 2, 3, 4).reshape(K, FB, BLK, BLK).astype(jnp.float32)
        outw_full = outw_parts.transpose(1, 0, 2, 3, 4).reshape(K, FB, BLK, BLK).astype(jnp.float32)
        return ((totals[0] + in_full, totals[1] + outw_full), (out_sum.astype(jnp.bfloat16), token_sum.astype(jnp.bfloat16)))
    start_sums = (jnp.zeros((K, FB, BLK, BLK), jnp.float32), jnp.zeros((K, FB, BLK, BLK), jnp.float32))
    (in_grad, out_grad), (mixed, token_grad) = lax.scan(group_step, start_sums, (group_in, group_back))
    return (mixed.reshape(TOKENS, MODEL_WIDTH), token_grad.reshape(TOKENS, MODEL_WIDTH), in_grad, out_grad)
```

```python
import functools
import math

import jax
import jax.numpy as jnp
from jax import lax
from jax.experimental import pallas as pl
from jax.experimental.pallas import tpu as pltpu
from jax.sharding import PartitionSpec as P

MESH = pl.DeviceIdType.MESH
gelu_root = 0.7978845608028654
gelu_cubic = 0.044715

BLK = 128
DB = 32
SLOTS = 16
COLS = 8
ROWS = 24
PAIR = 2 * ROWS
HALF = DB // 2
F32 = jnp.float32
BF16 = jnp.bfloat16

Z_FULL = (0, 1)
Z_HALF = (2, 3)
Y_FULL = ((4, 5), (8, 9), (12, 13), (16, 17))
Y_HALF = ((6, 7), (10, 11), (14, 15), (18, 19))
OY_HALF = ((20, 21), (24, 25), (28, 29), (32, 33))
OY_FULL = ((22, 23), (26, 27), (30, 31), (34, 35))
OZ_HALF = (36, 37)
OZ_FULL = (38, 39)
CORE = 40
XHALF = (48, 56)
XFULL = (64, 72)
ZLO = 80
COPIES = 88


def gelu_parts(pre):
    argument = gelu_root * (pre + gelu_cubic * pre * pre * pre)
    tangent = jnp.tanh(argument)
    activated = 0.5 * pre * (1.0 + tangent)
    slope = 0.5 * (1.0 + tangent) + 0.5 * pre * (1.0 - tangent * tangent) * gelu_root * (
        1.0 + 3.0 * gelu_cubic * pre * pre
    )
    return (activated, slope)


def kernel(
    grad_scale,
    slot_ref, live_ref, inverse_ref,
    tok_ref, cot_ref, w_in_ref, w_out_ref,
    mixed_ref, tgrad_ref, igrad_ref, ograd_ref,
    x0, x1, x2, x3,
    o0, o1, o2, o3,
    w_fwd, w_outz, w_inz, w_raw,
    hid, pgr, gmat,
    wg, core_in, xa, xb, xf1, xf2, zr,
    ya, yb, yf1, yf2, za, zb, zf1, zf2,
    load_sem, ssem, rsem,
):
    X = (x0, x1, x2, x3)
    O = (o0, o1, o2, o3)
    dp = lax.axis_index("dp")
    hd = lax.axis_index("hid")
    x, zl, core = dp // 4, lax.rem(dp // 2, 2), lax.rem(dp, 2)
    y, zh = hd // 4, lax.rem(hd, 4)

    def dev(dx=0, dzl=0, dcore=0, dy=0, dzh=0):
        return (
            lax.rem(x + dx + 4, 4) * 4 + lax.rem(zl + dzl, 2) * 2 + lax.rem(core + dcore, 2),
            lax.rem(y + dy + 4, 4) * 4 + lax.rem(zh + dzh + 4, 4),
        )

    zp, zm, yp, ym = dev(dzh=1), dev(dzh=-1), dev(dy=1), dev(dy=-1)
    xp, xm, other_zl, other_core = dev(dx=1), dev(dx=-1), dev(dzl=1), dev(dcore=1)

    def rcopy(src, dst, i, to):
        return pltpu.make_async_remote_copy(
            src_ref=src, dst_ref=dst, send_sem=ssem.at[i], recv_sem=rsem.at[i],
            device_id=to, device_id_type=MESH,
        )

    out_load = pltpu.make_async_copy(w_out_ref, w_outz.at[pl.ds(0, SLOTS)], load_sem.at[2])
    out_load.start()

    def in_load(k, slot):
        return pltpu.make_async_copy(w_in_ref.at[k], w_raw.at[slot], load_sem.at[slot])

    in_load(0, 0).start()

    barrier = pltpu.get_barrier_semaphore()
    peers = (zp, zm, yp, ym, xp, xm, other_zl, other_core)
    for p in peers:
        pl.semaphore_signal(barrier, inc=1, device_id=p, device_id_type=MESH)

    for b in range(DB):
        cols = pl.ds(b * BLK, BLK)
        both = jnp.concatenate(
            [tok_ref[:, cols].astype(F32), cot_ref[:, cols].astype(F32)], axis=0
        )
        x0[0, b] = both.astype(BF16)
    pl.semaphore_wait(barrier, len(peers))

    lo, hi = pl.ds(0, HALF), pl.ds(HALF, HALF)

    z_full = (
        rcopy(x0.at[0], x1.at[0], Z_FULL[0], zp),
        rcopy(x0.at[0], x2.at[0], Z_FULL[1], zm),
    )
    z_half = (
        rcopy(x1.at[0, lo], x3.at[0, lo], Z_HALF[0], zp),
        rcopy(x2.at[0, hi], x3.at[0, hi], Z_HALF[1], zm),
    )
    y_full = [
        (
            rcopy(X[j].at[0], X[j].at[1], Y_FULL[j][0], yp),
            rcopy(X[j].at[0], X[j].at[2], Y_FULL[j][1], ym),
        )
        for j in range(4)
    ]
    y_half = [
        (
            rcopy(X[j].at[1, lo], X[j].at[3, lo], Y_HALF[j][0], yp),
            rcopy(X[j].at[2, hi], X[j].at[3, hi], Y_HALF[j][1], ym),
        )
        for j in range(4)
    ]

    def start(pair):
        for c in pair:
            c.start()

    def arrived(pair):
        for c in pair:
            c.wait_recv()

    def forward_y(j):
        for full, half in zip(y_full[j], y_half[j]):
            full.wait_recv()
            half.start()

    def prepare(k, _):
        slot = lax.rem(k, 2)
        in_load(k, slot).wait()

        @pl.when(k + 1 < SLOTS)
        def _():
            in_load(k + 1, 1 - slot).start()

        for c in range(COLS):
            live = live_ref[k, c]
            wi = (w_raw[slot, c].astype(F32) * live).astype(BF16)
            wo = (w_outz[k, c].astype(F32) * live).astype(BF16)
            w_outz[k, c] = wo
            w_inz[k, c] = wi.T
            w_fwd[c, pl.ds(k * BLK, BLK), :] = jnp.concatenate([wi, wo.T], axis=1)
        return 0

    def forward(j):
        def one(c, _):
            lhs = jnp.concatenate(
                [X[j][:, slot_ref[k, c]].reshape(4 * PAIR, BLK) for k in range(SLOTS)], axis=1
            )
            acc = jnp.dot(lhs, w_fwd[c], preferred_element_type=F32)
            acc = acc.reshape(4, PAIR, 2 * BLK)
            pre = acc[:, :ROWS, :BLK]
            hidden_grad = acc[:, ROWS:, BLK:]
            activated, slope = gelu_parts(pre)
            pre_grad = hidden_grad * slope
            rows = pl.ds(j * 4 * ROWS, 4 * ROWS)
            hid[c, rows, :] = activated.reshape(4 * ROWS, BLK).astype(BF16)
            pgr[c, rows, :] = pre_grad.reshape(4 * ROWS, BLK).astype(BF16)
            zero = jnp.zeros_like(pre)
            both = jnp.concatenate(
                [
                    jnp.concatenate([pre_grad, zero], axis=2),
                    jnp.concatenate([zero, activated], axis=2),
                ],
                axis=1,
            )
            gmat[c, pl.ds(j * 4 * PAIR, 4 * PAIR), :] = both.reshape(4 * PAIR, 2 * BLK).astype(BF16)
            return 0

        lax.fori_loop(0, COLS, one, 0)

    start(z_full)
    start(y_full[0])
    w_outz[SLOTS] = jnp.zeros(w_outz.shape[1:], BF16)
    w_inz[SLOTS] = jnp.zeros(w_inz.shape[1:], BF16)
    out_load.wait()
    lax.fori_loop(0, SLOTS // 2, prepare, 0)
    forward_y(0)
    lax.fori_loop(SLOTS // 2, SLOTS, prepare, 0)
    for full, half in zip(z_full, z_half):
        full.wait_recv()
        half.start()
    start(y_full[1])
    start(y_full[2])
    arrived(y_half[0])
    forward(0)
    forward_y(1)
    arrived(z_half)
    start(y_full[3])
    forward_y(2)
    arrived(y_half[1])
    forward(1)
    arrived(y_half[2])
    forward(2)
    forward_y(3)
    arrived(y_half[3])
    forward(3)

    steps = (0, 3, 1, 2)

    def core_copy(c):
        return rcopy(wg.at[1, c], core_in.at[c], CORE + c, other_core)

    def x_half(c):
        return (
            rcopy(wg.at[0, c, 6], xa.at[c], XHALF[0] + c, xm),
            rcopy(wg.at[0, c, 7], xb.at[c], XHALF[1] + c, xp),
        )

    def x_full(c):
        return (
            rcopy(wg.at[0, c, pl.ds(2, 2)], xf1.at[c], XFULL[0] + c, xm),
            rcopy(wg.at[0, c, pl.ds(4, 2)], xf2.at[c], XFULL[1] + c, xp),
        )

    def z_low(c):
        return rcopy(wg.at[0, c, 1], zr.at[c], ZLO + c, other_zl)

    def weight_grad(c, _):
        left = gmat[c].T
        for rc in (1, 0):
            for rx in range(4):
                tiles, masks = [], []
                for rz in range(2):
                    k = (
                        lax.rem(x + steps[rx], 4) * 4
                        + lax.rem(zl + rz, 2) * 2
                        + lax.rem(core + rc, 2)
                    )
                    b = slot_ref[k, c]
                    tiles.append(
                        jnp.concatenate([X[j][:, b].reshape(4 * PAIR, BLK) for j in range(4)], axis=0)
                    )
                    masks.append(live_ref[k, c] * grad_scale)
                res = jnp.dot(left, jnp.concatenate(tiles, axis=1), preferred_element_type=F32)
                for rz in range(2):
                    wg[rc, c, rx * 2 + rz] = (
                        res[:, rz * BLK : (rz + 1) * BLK] * masks[rz]
                    ).astype(BF16)
            if rc == 1:
                core_copy(c).start()
        return 0

    def add_core(c):
        core_copy(c).wait_recv()
        for i in (6, 7, 2, 3, 4, 5, 0, 1):
            wg[0, c, i] = (wg[0, c, i].astype(F32) + core_in[c, i].astype(F32)).astype(BF16)
        start(x_half(c))

    def add_x_half(c):
        arrived(x_half(c))
        wg[0, c, 2] = (wg[0, c, 2].astype(F32) + xa[c].astype(F32)).astype(BF16)
        wg[0, c, 5] = (wg[0, c, 5].astype(F32) + xb[c].astype(F32)).astype(BF16)
        start(x_full(c))

    def add_x_full(c):
        arrived(x_full(c))
        wg[0, c, 1] = (
            wg[0, c, 1].astype(F32) + xf1[c, 1].astype(F32) + xf2[c, 1].astype(F32)
        ).astype(BF16)
        z_low(c).start()

    def finish(c):
        z_low(c).wait_recv()
        total = (
            wg[0, c, 0].astype(F32) + xf1[c, 0].astype(F32) + xf2[c, 0].astype(F32)
            + zr[c].astype(F32)
        )
        igrad_ref[0, c] = total[:BLK].T
        ograd_ref[0, c] = total[BLK:]

    def loop(f, first, last):
        def step(c, _):
            f(c)
            return 0

        lax.fori_loop(first, last, step, 0)

    lax.fori_loop(0, COLS, weight_grad, 0)
    loop(add_core, 0, COLS)

    def spread(q, _):
        def placed(source):
            return jnp.concatenate(
                [
                    jnp.concatenate(
                        [source[inverse_ref[c, 2 * q], c], source[inverse_ref[c, 2 * q + 1], c]],
                        axis=1,
                    )
                    for c in range(COLS)
                ],
                axis=0,
            )

        h = jnp.concatenate([hid[c] for c in range(COLS)], axis=1)
        g = jnp.concatenate([pgr[c] for c in range(COLS)], axis=1)
        m = jnp.dot(h, placed(w_outz), preferred_element_type=F32).reshape(16, ROWS, 2 * BLK)
        t = jnp.dot(g, placed(w_inz), preferred_element_type=F32).reshape(16, ROWS, 2 * BLK)
        both = jnp.concatenate([m, t], axis=1).astype(BF16)
        for j in range(4):
            for i in range(2):
                O[j][:, 2 * q + i] = both[4 * j : 4 * j + 4, :, i * BLK : (i + 1) * BLK]
        return 0

    lax.fori_loop(0, DB // 2, spread, 0)

    def add_blocks(dst, d, src, s, first, count):
        def step(i, _):
            at = pl.ds(first + i * 8, 8)
            frm = pl.ds(i * 8, 8)
            dst[d, at] = (dst[d, at].astype(F32) + src[s, frm].astype(F32)).astype(BF16)
            return 0

        lax.fori_loop(0, count // 8, step, 0)

    oy_half = [
        (
            rcopy(O[j].at[3, lo], ya.at[j], OY_HALF[j][0], ym),
            rcopy(O[j].at[3, hi], yb.at[j], OY_HALF[j][1], yp),
        )
        for j in range(4)
    ]
    oy_full = [
        (
            rcopy(O[j].at[1], yf1.at[j], OY_FULL[j][0], ym),
            rcopy(O[j].at[2], yf2.at[j], OY_FULL[j][1], yp),
        )
        for j in range(4)
    ]
    oz_half = (
        rcopy(o3.at[0, lo], za.at[0], OZ_HALF[0], zm),
        rcopy(o3.at[0, hi], zb.at[0], OZ_HALF[1], zp),
    )
    oz_full = (
        rcopy(o1.at[0], zf1.at[0], OZ_FULL[0], zm),
        rcopy(o2.at[0], zf2.at[0], OZ_FULL[1], zp),
    )

    def y_mid(j):
        oy_half[j][0].wait_recv()
        add_blocks(O[j], 1, ya, j, 0, HALF)
        oy_full[j][0].start()
        oy_half[j][1].wait_recv()
        add_blocks(O[j], 2, yb, j, HALF, HALF)
        oy_full[j][1].start()

    def y_end(j):
        arrived(oy_full[j])
        add_blocks(O[j], 0, yf1, j, 0, DB)
        add_blocks(O[j], 0, yf2, j, 0, DB)

    for j in (3, 1, 2, 0):
        start(oy_half[j])
    loop(add_x_half, 0, COLS)
    y_mid(3)
    y_mid(1)
    y_end(3)
    start(oz_half)
    y_mid(2)
    y_end(1)
    oz_half[0].wait_recv()
    add_blocks(o1, 0, za, 0, 0, HALF)
    oz_full[0].start()
    y_mid(0)
    y_end(2)
    oz_half[1].wait_recv()
    add_blocks(o2, 0, zb, 0, HALF, HALF)
    oz_full[1].start()
    loop(add_x_full, 0, COLS)
    y_end(0)
    loop(finish, 0, COLS)
    arrived(oz_full)
    for b in range(DB):
        total = o0[0, b].astype(F32) + zf1[0, b].astype(F32) + zf2[0, b].astype(F32)
        cols = pl.ds(b * BLK, BLK)
        mixed_ref[:, cols] = total[:ROWS].astype(BF16)
        tgrad_ref[:, cols] = total[ROWS:].astype(BF16)

    for pair in (z_full, z_half, *y_full, *y_half, *oy_half, *oy_full, oz_half, oz_full):
        for c in pair:
            c.wait_send()

    def sent(c):
        core_copy(c).wait_send()
        for r in (*x_half(c), *x_full(c)):
            r.wait_send()
        z_low(c).wait_send()

    loop(sent, 0, COLS)


def body(tokens, cotangent, w_in, w_out, block_index, live_count):
    slots, columns = block_index.shape
    grad_scale = 1.0 / math.sqrt(tokens.shape[0] * lax.axis_size("hid") * lax.axis_size("dp"))
    slot_number = lax.broadcasted_iota(jnp.int32, (slots, columns), 0)
    active = slot_number < live_count[None, :]
    slot = jnp.where(active, block_index, 0)
    hit = active[:, :, None] & (
        block_index[:, :, None] == lax.broadcasted_iota(jnp.int32, (slots, columns, DB), 2)
    )
    inverse = slots + jnp.sum(jnp.where(hit, slot_number[:, :, None] - slots, 0), axis=0)
    vmem = pl.BlockSpec(memory_space=pltpu.VMEM)
    smem = pl.BlockSpec(memory_space=pltpu.SMEM)
    hbm = pl.BlockSpec(memory_space=pl.ANY)
    shard = (4, DB, PAIR, BLK)
    half = (HALF, PAIR, BLK)
    full = (DB, PAIR, BLK)
    return pl.pallas_call(
        functools.partial(kernel, grad_scale),
        out_shape=(
            jax.ShapeDtypeStruct(tokens.shape, BF16),
            jax.ShapeDtypeStruct(tokens.shape, BF16),
            jax.ShapeDtypeStruct((1, COLS, BLK, BLK), F32),
            jax.ShapeDtypeStruct((1, COLS, BLK, BLK), F32),
        ),
        in_specs=[smem, smem, smem, vmem, vmem, hbm, hbm],
        out_specs=(vmem, vmem, vmem, vmem),
        scratch_shapes=[
            *[pltpu.VMEM(shard, BF16) for _ in range(8)],
            pltpu.VMEM((COLS, SLOTS * BLK, 2 * BLK), BF16),
            pltpu.VMEM((SLOTS + 1, COLS, BLK, BLK), BF16),
            pltpu.VMEM((SLOTS + 1, COLS, BLK, BLK), BF16),
            pltpu.VMEM((2, COLS, BLK, BLK), BF16),
            pltpu.VMEM((COLS, 16 * ROWS, BLK), BF16),
            pltpu.VMEM((COLS, 16 * ROWS, BLK), BF16),
            pltpu.VMEM((COLS, 16 * PAIR, 2 * BLK), BF16),
            pltpu.VMEM((2, COLS, 8, 2 * BLK, BLK), BF16),
            pltpu.VMEM((COLS, 8, 2 * BLK, BLK), BF16),
            pltpu.VMEM((COLS, 2 * BLK, BLK), BF16),
            pltpu.VMEM((COLS, 2 * BLK, BLK), BF16),
            pltpu.VMEM((COLS, 2, 2 * BLK, BLK), BF16),
            pltpu.VMEM((COLS, 2, 2 * BLK, BLK), BF16),
            pltpu.VMEM((COLS, 2 * BLK, BLK), BF16),
            pltpu.VMEM((4, *half), BF16),
            pltpu.VMEM((4, *half), BF16),
            pltpu.VMEM((4, *full), BF16),
            pltpu.VMEM((4, *full), BF16),
            pltpu.VMEM((1, *half), BF16),
            pltpu.VMEM((1, *half), BF16),
            pltpu.VMEM((1, *full), BF16),
            pltpu.VMEM((1, *full), BF16),
            pltpu.SemaphoreType.DMA((3,)),
            pltpu.SemaphoreType.DMA((COPIES,)),
            pltpu.SemaphoreType.DMA((COPIES,)),
        ],
        compiler_params=pltpu.CompilerParams(
            collective_id=0, has_side_effects=True, vmem_limit_bytes=62 * 2**20
        ),
        cost_estimate=pl.CostEstimate(
            flops=3 * 2 * 2 * 384 * 2048 * 1024, bytes_accessed=12 * 2**20, transcendentals=384 * 1024
        ),
    )(slot, active.astype(F32), inverse, tokens, cotangent, w_in, w_out)


def solution(mesh):
    in_specs = (
        P(("dp", "hid"), None),
        P(("dp", "hid"), None),
        P(None, "hid", None, None),
        P(None, "hid", None, None),
        P(None, "hid"),
        P("hid"),
    )
    out_specs = (
        P(("dp", "hid"), None),
        P(("dp", "hid"), None),
        P("dp", "hid", None, None),
        P("dp", "hid", None, None),
    )
    return jax.shard_map(body, mesh=mesh, in_specs=in_specs, out_specs=out_specs, check_vma=False)
```

```python
import functools
import math

import jax
import jax.numpy as jnp
from jax import lax
from jax.experimental import pallas as pl
from jax.experimental.pallas import tpu as pltpu
from jax.sharding import PartitionSpec as P

MESH = pl.DeviceIdType.MESH
gelu_root = 0.7978845608028654
gelu_cubic = 0.044715

BLK = 128
DB = 32
SLOTS = 16
COLS = 8
ROWS = 24
PAIR = 2 * ROWS
HALF = DB // 2
F32 = jnp.float32
BF16 = jnp.bfloat16

GROUPS = (
    ((0, 0), (0, 1), (0, 2), (0, 3)),
    ((1, 0), (1, 1), (1, 2), (2, 0), (2, 1), (2, 2)),
    ((3, 0), (3, 1), (3, 2), (3, 3), (1, 3), (2, 3)),
)
PLACE = {jr: (g, i) for g, group in enumerate(GROUPS) for i, jr in enumerate(group)}
ORDER = {jr: n for n, jr in enumerate(jr for group in GROUPS for jr in group)}
FIRST = (0, 4, 10)
COPIES = 112


def gelu_parts(pre):
    argument = gelu_root * (pre + gelu_cubic * pre * pre * pre)
    tangent = jnp.tanh(argument)
    activated = 0.5 * pre * (1.0 + tangent)
    slope = 0.5 * (1.0 + tangent) + 0.5 * pre * (1.0 - tangent * tangent) * gelu_root * (
        1.0 + 3.0 * gelu_cubic * pre * pre
    )
    return (activated, slope)


def kernel(
    grad_scale,
    index_ref, count_ref,
    tok_ref, cot_ref, w_in_ref, w_out_ref,
    mixed_ref, tgrad_ref, igrad_ref, ograd_ref,
    x0, x1, x2, parts,
    w_fwd, w_outz, w_inz,
    hid, pgr, gmat,
    wg, core_in, xa, xb, xf1, xf2, zr,
    ya, yb, yf1, yf2, za, zb, zf1, zf2, zq1, zq2,
    inverse,
    load_sem, ssem, rsem,
):
    X = (x0, x1, x2)
    dp = lax.axis_index("dp")
    hd = lax.axis_index("hid")
    x, zl, core = dp // 4, lax.rem(dp // 2, 2), lax.rem(dp, 2)
    y, zh = hd // 4, lax.rem(hd, 4)

    def dev(dx=0, dzl=0, dcore=0, dy=0, dzh=0):
        return (
            lax.rem(x + dx + 4, 4) * 4 + lax.rem(zl + dzl, 2) * 2 + lax.rem(core + dcore, 2),
            lax.rem(y + dy + 4, 4) * 4 + lax.rem(zh + dzh + 4, 4),
        )

    zp, zm, yp, ym = dev(dzh=1), dev(dzh=-1), dev(dy=1), dev(dy=-1)
    xp, xm, other_zl, other_core = dev(dx=1), dev(dx=-1), dev(dzl=1), dev(dcore=1)

    copies = []
    numbers = iter(range(COPIES))

    def make(src, dst, i, to):
        return pltpu.make_async_remote_copy(
            src_ref=src, dst_ref=dst, send_sem=ssem.at[i], recv_sem=rsem.at[i],
            device_id=to, device_id_type=MESH,
        )

    def rcopy(src, dst, to):
        c = make(src, dst, next(numbers), to)
        copies.append(c)
        return c

    def start(pair):
        for c in pair:
            c.start()

    def arrived(pair):
        for c in pair:
            c.wait_recv()

    def live(k, c):
        return k < count_ref[c]

    def slot(k, c):
        return jnp.where(live(k, c), index_ref[c, k], 0)

    def mask(k, c):
        return jnp.where(live(k, c), 1.0, 0.0).astype(F32)

    def loop(f, first, last):
        def step(c, _):
            f(c)
            return 0

        lax.fori_loop(first, last, step, 0)

    def raw(k):
        return wg.at[k // 8, lax.rem(k, 8), :, pl.ds(0, BLK), :]

    def in_load(k):
        return pltpu.make_async_copy(w_in_ref.at[k], raw(k), load_sem.at[k])

    def out_load(k):
        return pltpu.make_async_copy(w_out_ref.at[k], w_outz.at[k], load_sem.at[SLOTS + k])

    barrier = pltpu.get_barrier_semaphore()
    peers = (zp, zm, yp, ym, xp, xm, other_zl, other_core)
    for p in peers:
        pl.semaphore_signal(barrier, inc=1, device_id=p, device_id_type=MESH)

    for b in range(DB):
        cols = pl.ds(b * BLK, BLK)
        both = jnp.concatenate(
            [tok_ref[:, cols].astype(F32), cot_ref[:, cols].astype(F32)], axis=0
        )
        x0[0, b] = both.astype(BF16)
    pl.semaphore_wait(barrier, len(peers))

    lo, hi = pl.ds(0, HALF), pl.ds(HALF, HALF)
    whole = pl.ds(0, DB)

    def shard(j, r, blocks=whole):
        g, i = PLACE[(j, r)]
        return X[g].at[i, blocks]

    def part(j, r, blocks=whole):
        return parts.at[ORDER[(j, r)], blocks]

    z_first = (
        rcopy(shard(0, 0, lo), shard(1, 0, lo), zp),
        rcopy(shard(0, 0, hi), shard(2, 0, hi), zm),
    )
    z_second = (
        rcopy(shard(0, 0, hi), shard(1, 0, hi), zp),
        rcopy(shard(0, 0, lo), shard(2, 0, lo), zm),
    )
    z_relay = (
        rcopy(shard(1, 0, lo), shard(3, 0, lo), zp),
        rcopy(shard(2, 0, hi), shard(3, 0, hi), zm),
    )
    z_cross = (
        rcopy(shard(0, 3), shard(1, 3), zp),
        rcopy(shard(0, 3), shard(2, 3), zm),
    )

    def both_ways(j, blocks):
        return (
            rcopy(shard(j, 0, blocks), shard(j, 1, blocks), yp),
            rcopy(shard(j, 0, blocks), shard(j, 2, blocks), ym),
        )

    def y_relay_of(j):
        return (
            rcopy(shard(j, 1, lo), shard(j, 3, lo), yp),
            rcopy(shard(j, 2, hi), shard(j, 3, hi), ym),
        )

    y_own = both_ways(0, whole)
    y_one = (both_ways(1, lo), both_ways(1, hi))
    y_two = (both_ways(2, hi), both_ways(2, lo))
    y_far = (both_ways(3, lo), both_ways(3, hi))
    y_relay_own = y_relay_of(0)
    y_relay_far = y_relay_of(3)

    def prepare(k):
        in_load(k).wait()
        out_load(k).wait()
        for c in range(COLS):
            m = mask(k, c)
            wi = (wg[k // 8, lax.rem(k, 8), c, :BLK, :].astype(F32) * m).astype(BF16)
            wo = (w_outz[k, c].astype(F32) * m).astype(BF16)
            w_outz[k, c] = wo
            w_inz[k, c] = wi.T
            w_fwd[c, pl.ds(k * BLK, BLK), :] = jnp.concatenate([wi, wo.T], axis=1)

    def invert(c):
        joined = [jnp.where(live(k, c), index_ref[c, k], -1) for k in range(SLOTS)]

        def one(b):
            found = jnp.int32(SLOTS)
            for k in range(SLOTS):
                found = jnp.where(joined[k] == b, k, found)
            inverse[c, b] = found

        loop(one, 0, DB)

    def forward(g):
        n = len(GROUPS[g])

        def one(c):
            lhs = jnp.concatenate(
                [X[g][:, slot(k, c)].reshape(n * PAIR, BLK) for k in range(SLOTS)], axis=1
            )
            acc = jnp.dot(lhs, w_fwd[c], preferred_element_type=F32)
            acc = acc.reshape(n, PAIR, 2 * BLK)
            pre = acc[:, :ROWS, :BLK]
            hidden_grad = acc[:, ROWS:, BLK:]
            activated, slope = gelu_parts(pre)
            pre_grad = hidden_grad * slope
            rows = pl.ds(FIRST[g] * ROWS, n * ROWS)
            hid[c, rows, :] = activated.reshape(n * ROWS, BLK).astype(BF16)
            pgr[c, rows, :] = pre_grad.reshape(n * ROWS, BLK).astype(BF16)
            zero = jnp.zeros_like(pre)
            both = jnp.concatenate(
                [
                    jnp.concatenate([pre_grad, zero], axis=2),
                    jnp.concatenate([zero, activated], axis=2),
                ],
                axis=1,
            )
            gmat[c, pl.ds(FIRST[g] * PAIR, n * PAIR), :] = both.reshape(n * PAIR, 2 * BLK).astype(BF16)

        loop(one, 0, COLS)

    def spread(first, count):
        rows = pl.ds(first * ROWS, count * ROWS)

        def one(q):
            def placed(source):
                return jnp.concatenate(
                    [
                        jnp.concatenate(
                            [source[inverse[c, 2 * q], c], source[inverse[c, 2 * q + 1], c]],
                            axis=1,
                        )
                        for c in range(COLS)
                    ],
                    axis=0,
                )

            h = jnp.concatenate([hid[c, rows, :] for c in range(COLS)], axis=1)
            g = jnp.concatenate([pgr[c, rows, :] for c in range(COLS)], axis=1)
            m = jnp.dot(h, placed(w_outz), preferred_element_type=F32)
            t = jnp.dot(g, placed(w_inz), preferred_element_type=F32)
            both = jnp.concatenate(
                [m.reshape(count, ROWS, 2 * BLK), t.reshape(count, ROWS, 2 * BLK)], axis=1
            ).astype(BF16)
            for i in range(2):
                parts[pl.ds(first, count), 2 * q + i] = both[:, :, i * BLK : (i + 1) * BLK]

        loop(one, 0, DB // 2)

    start(z_first)
    start(y_own)
    start(z_second)
    for k in range(SLOTS):
        in_load(k).start()
        out_load(k).start()
    w_outz[SLOTS] = jnp.zeros(w_outz.shape[1:], BF16)
    w_inz[SLOTS] = jnp.zeros(w_inz.shape[1:], BF16)
    loop(prepare, 0, SLOTS // 2)
    arrived(y_own)
    start(y_relay_own)
    arrived(z_first)
    start(z_relay)
    start(y_one[0])
    start(y_two[0])
    loop(prepare, SLOTS // 2, SLOTS)
    arrived(y_relay_own)
    start(z_cross)
    loop(invert, 0, COLS)
    arrived(z_second)
    start(y_one[1])
    start(y_two[1])
    forward(0)
    arrived(z_relay)
    start(y_far[0])
    start(y_far[1])
    for pair in (*y_one, *y_two):
        arrived(pair)
    forward(1)
    spread(0, 10)

    def add_blocks(dst, src, first, count):
        def step(i):
            at = pl.ds(first + i * 8, 8)
            frm = pl.ds(i * 8, 8)
            n = ORDER[dst]
            parts[n, at] = (parts[n, at].astype(F32) + src[frm].astype(F32)).astype(BF16)

        loop(step, 0, count // 8)

    oz_cross = (
        rcopy(part(1, 3), zq1.at[whole], zm),
        rcopy(part(2, 3), zq2.at[whole], zp),
    )
    oy_half = {
        j: (
            rcopy(part(j, 3, lo), ya.at[n], ym),
            rcopy(part(j, 3, hi), yb.at[n], yp),
        )
        for n, j in enumerate((0, 3))
    }
    oy_full = {
        j: (
            rcopy(part(j, 1), yf1.at[j], ym),
            rcopy(part(j, 2), yf2.at[j], yp),
        )
        for j in range(4)
    }
    oz_half = (
        rcopy(part(3, 0, lo), za.at[lo], zm),
        rcopy(part(3, 0, hi), zb.at[lo], zp),
    )
    oz_full = (
        rcopy(part(1, 0), zf1.at[whole], zm),
        rcopy(part(2, 0), zf2.at[whole], zp),
    )

    def y_mid(j):
        n = (0, 3).index(j)
        oy_half[j][0].wait_recv()
        add_blocks((j, 1), ya.at[n], 0, HALF)
        oy_full[j][0].start()
        oy_half[j][1].wait_recv()
        add_blocks((j, 2), yb.at[n], HALF, HALF)
        oy_full[j][1].start()

    def y_end(j):
        arrived(oy_full[j])
        add_blocks((j, 0), yf1.at[j], 0, DB)
        add_blocks((j, 0), yf2.at[j], 0, DB)

    y_far[0][0].wait_recv()
    y_relay_far[0].start()
    y_far[1][1].wait_recv()
    y_relay_far[1].start()
    start(oy_full[1])
    start(oy_full[2])
    y_far[0][1].wait_recv()
    y_far[1][0].wait_recv()
    arrived(z_cross)
    arrived(y_relay_far)
    forward(2)
    spread(10, 6)
    start(oz_cross)
    start(oy_half[3])

    steps = (0, 3, 1, 2)
    base = len(copies)
    CORE, XH1, XH2, XF1, XF2, ZLO = (base + 8 * i for i in range(6))

    def core_copy(c):
        return make(wg.at[1, c], core_in.at[c], CORE + c, other_core)

    def x_half(c):
        return (
            make(wg.at[0, c, 6], xa.at[c], XH1 + c, xm),
            make(wg.at[0, c, 7], xb.at[c], XH2 + c, xp),
        )

    def x_full(c):
        return (
            make(wg.at[0, c, pl.ds(2, 2)], xf1.at[c], XF1 + c, xm),
            make(wg.at[0, c, pl.ds(4, 2)], xf2.at[c], XF2 + c, xp),
        )

    def z_low(c):
        return make(wg.at[0, c, 1], zr.at[c], ZLO + c, other_zl)

    def add_core(c):
        core_copy(c).wait_recv()
        for i in (6, 7, 2, 3, 4, 5, 0, 1):
            wg[0, c, i] = (wg[0, c, i].astype(F32) + core_in[c, i].astype(F32)).astype(BF16)
        start(x_half(c))

    def add_x_half(c):
        arrived(x_half(c))
        wg[0, c, 2] = (wg[0, c, 2].astype(F32) + xa[c].astype(F32)).astype(BF16)
        wg[0, c, 5] = (wg[0, c, 5].astype(F32) + xb[c].astype(F32)).astype(BF16)
        start(x_full(c))

    def add_x_full(c):
        arrived(x_full(c))
        wg[0, c, 1] = (
            wg[0, c, 1].astype(F32) + xf1[c, 1].astype(F32) + xf2[c, 1].astype(F32)
        ).astype(BF16)
        z_low(c).start()

    def finish(c):
        z_low(c).wait_recv()
        total = (
            wg[0, c, 0].astype(F32) + xf1[c, 0].astype(F32) + xf2[c, 0].astype(F32)
            + zr[c].astype(F32)
        )
        igrad_ref[0, c] = total[:BLK].T
        ograd_ref[0, c] = total[BLK:]

    def weight_grad(c):
        left = gmat[c].T
        for rc in (1, 0):
            for rx in range(4):
                tiles, masks = [], []
                for rz in range(2):
                    k = (
                        lax.rem(x + steps[rx], 4) * 4
                        + lax.rem(zl + rz, 2) * 2
                        + lax.rem(core + rc, 2)
                    )
                    b = slot(k, c)
                    tiles.append(
                        jnp.concatenate(
                            [X[g][:, b].reshape(len(GROUPS[g]) * PAIR, BLK) for g in range(3)], axis=0
                        )
                    )
                    masks.append(mask(k, c) * grad_scale)
                res = jnp.dot(left, jnp.concatenate(tiles, axis=1), preferred_element_type=F32)
                for rz in range(2):
                    wg[rc, c, rx * 2 + rz] = (
                        res[:, rz * BLK : (rz + 1) * BLK] * masks[rz]
                    ).astype(BF16)
            if rc == 1:
                core_copy(c).start()

        @pl.when(c >= 1)
        def _():
            add_core(c - 1)

        @pl.when(c >= 4)
        def _():
            add_x_half(c - 4)

        @pl.when(c == 5)
        def _():
            y_mid(3)

    loop(weight_grad, 0, COLS)
    add_core(COLS - 1)
    loop(add_x_half, 4, COLS)
    y_end(1)
    y_end(2)
    arrived(oz_cross)
    add_blocks((0, 3), zq1, 0, DB)
    add_blocks((0, 3), zq2, 0, DB)
    start(oy_half[0])
    y_end(3)
    start(oz_half)
    loop(add_x_full, 0, 3)
    y_mid(0)
    oz_half[0].wait_recv()
    add_blocks((1, 0), za, 0, HALF)
    oz_full[0].start()
    oz_half[1].wait_recv()
    add_blocks((2, 0), zb, HALF, HALF)
    oz_full[1].start()
    loop(add_x_full, 3, COLS)
    y_end(0)
    loop(finish, 0, COLS)
    arrived(oz_full)
    for b in range(DB):
        total = parts[0, b].astype(F32) + zf1[b].astype(F32) + zf2[b].astype(F32)
        cols = pl.ds(b * BLK, BLK)
        mixed_ref[:, cols] = total[:ROWS].astype(BF16)
        tgrad_ref[:, cols] = total[ROWS:].astype(BF16)

    for c in copies:
        c.wait_send()

    def sent(c):
        core_copy(c).wait_send()
        for r in (*x_half(c), *x_full(c)):
            r.wait_send()
        z_low(c).wait_send()

    loop(sent, 0, COLS)


def hand_on(*refs):
    n = len(refs) // 2
    for i in range(n):
        refs[n + i][...] = refs[i][...]


def body(tokens, cotangent, w_in, w_out, block_index, live_count):
    grad_scale = 1.0 / math.sqrt(tokens.shape[0] * lax.axis_size("hid") * lax.axis_size("dp"))
    vmem = pl.BlockSpec(memory_space=pltpu.VMEM)
    smem = pl.BlockSpec(memory_space=pltpu.SMEM)
    hbm = pl.BlockSpec(memory_space=pl.ANY)
    half = (HALF, PAIR, BLK)
    full = (DB, PAIR, BLK)
    tile = (2 * BLK, BLK)
    shapes = (
        jax.ShapeDtypeStruct(tokens.shape, BF16),
        jax.ShapeDtypeStruct(tokens.shape, BF16),
        jax.ShapeDtypeStruct((1, COLS, BLK, BLK), F32),
        jax.ShapeDtypeStruct((1, COLS, BLK, BLK), F32),
    )
    results = pl.pallas_call(
        functools.partial(kernel, grad_scale),
        out_shape=shapes,
        in_specs=[smem, smem, vmem, vmem, hbm, hbm],
        out_specs=(vmem, vmem, vmem, vmem),
        scratch_shapes=[
            *[pltpu.VMEM((len(g), *full), BF16) for g in GROUPS],
            pltpu.VMEM((16, *full), BF16),
            pltpu.VMEM((COLS, SLOTS * BLK, 2 * BLK), BF16),
            pltpu.VMEM((SLOTS + 1, COLS, BLK, BLK), BF16),
            pltpu.VMEM((SLOTS + 1, COLS, BLK, BLK), BF16),
            pltpu.VMEM((COLS, 16 * ROWS, BLK), BF16),
            pltpu.VMEM((COLS, 16 * ROWS, BLK), BF16),
            pltpu.VMEM((COLS, 16 * PAIR, 2 * BLK), BF16),
            pltpu.VMEM((2, COLS, 8, *tile), BF16),
            pltpu.VMEM((COLS, 8, *tile), BF16),
            pltpu.VMEM((COLS, *tile), BF16),
            pltpu.VMEM((COLS, *tile), BF16),
            pltpu.VMEM((COLS, 2, *tile), BF16),
            pltpu.VMEM((COLS, 2, *tile), BF16),
            pltpu.VMEM((COLS, *tile), BF16),
            pltpu.VMEM((2, *half), BF16),
            pltpu.VMEM((2, *half), BF16),
            pltpu.VMEM((4, *full), BF16),
            pltpu.VMEM((4, *full), BF16),
            pltpu.VMEM(half, BF16),
            pltpu.VMEM(half, BF16),
            *[pltpu.VMEM(full, BF16) for _ in range(4)],
            pltpu.SMEM((COLS, DB), jnp.int32),
            pltpu.SemaphoreType.DMA((2 * SLOTS,)),
            pltpu.SemaphoreType.DMA((COPIES,)),
            pltpu.SemaphoreType.DMA((COPIES,)),
        ],
        compiler_params=pltpu.CompilerParams(
            collective_id=0, has_side_effects=True, vmem_limit_bytes=62 * 2**20
        ),
        cost_estimate=pl.CostEstimate(
            flops=3 * 2 * 2 * 384 * 2048 * 1024, bytes_accessed=12 * 2**20, transcendentals=384 * 1024
        ),
    )(block_index.T, live_count, tokens, cotangent, w_in, w_out)
    return pl.pallas_call(
        hand_on,
        out_shape=shapes,
        in_specs=[vmem] * len(shapes),
        out_specs=(vmem,) * len(shapes),
    )(*results)


def solution(mesh):
    in_specs = (
        P(("dp", "hid"), None),
        P(("dp", "hid"), None),
        P(None, "hid", None, None),
        P(None, "hid", None, None),
        P(None, "hid"),
        P("hid"),
    )
    out_specs = (
        P(("dp", "hid"), None),
        P(("dp", "hid"), None),
        P("dp", "hid", None, None),
        P("dp", "hid", None, None),
    )
    return jax.shard_map(body, mesh=mesh, in_specs=in_specs, out_specs=out_specs, check_vma=False)
```

```python
import functools
import math

import jax
import jax.numpy as jnp
from jax import lax
from jax.experimental import pallas as pl
from jax.experimental.pallas import tpu as pltpu
from jax.sharding import PartitionSpec as P

MESH = pl.DeviceIdType.MESH
gelu_root = 0.7978845608028654
gelu_cubic = 0.044715

BLK = 128
DB = 32
SLOTS = 16
COLS = 8
ROWS = 24
PAIR = 2 * ROWS
HALF = DB // 2
F32 = jnp.float32
BF16 = jnp.bfloat16

GROUPS = (
    ((0, 0), (0, 1), (0, 2), (0, 3)),
    ((1, 0), (1, 1), (1, 2), (2, 0), (2, 1), (2, 2)),
    ((3, 0), (3, 1), (3, 2), (3, 3), (1, 3), (2, 3)),
)
PLACE = {jr: (g, i) for g, group in enumerate(GROUPS) for i, jr in enumerate(group)}
ORDER = {jr: n for n, jr in enumerate(jr for group in GROUPS for jr in group)}
FIRST = (0, 4, 10)
COPIES = 120


def gelu_parts(pre):
    argument = gelu_root * (pre + gelu_cubic * pre * pre * pre)
    tangent = jnp.tanh(argument)
    activated = 0.5 * pre * (1.0 + tangent)
    slope = 0.5 * (1.0 + tangent) + 0.5 * pre * (1.0 - tangent * tangent) * gelu_root * (
        1.0 + 3.0 * gelu_cubic * pre * pre
    )
    return (activated, slope)


def kernel(
    grad_scale,
    index_ref, count_ref,
    tok_ref, cot_ref, w_in_ref, w_out_ref,
    mixed_ref, tgrad_ref, igrad_ref, ograd_ref,
    x0, x1, x2, parts,
    w_fwd, w_outz, w_inz,
    hid, pgr, gmat,
    wg, core_in, xa, xb, xf1, xf2, zr,
    ya, yb, yf1, yf2, za, zb, zf1, zf2, zq1, zq2,
    inverse,
    load_sem, ssem, rsem,
):
    X = (x0, x1, x2)
    dp = lax.axis_index("dp")
    hd = lax.axis_index("hid")
    x, zl, core = dp // 4, lax.rem(dp // 2, 2), lax.rem(dp, 2)
    y, zh = hd // 4, lax.rem(hd, 4)

    def dev(dx=0, dzl=0, dcore=0, dy=0, dzh=0):
        return (
            lax.rem(x + dx + 4, 4) * 4 + lax.rem(zl + dzl, 2) * 2 + lax.rem(core + dcore, 2),
            lax.rem(y + dy + 4, 4) * 4 + lax.rem(zh + dzh + 4, 4),
        )

    zp, zm, yp, ym = dev(dzh=1), dev(dzh=-1), dev(dy=1), dev(dy=-1)
    xp, xm, other_zl, other_core = dev(dx=1), dev(dx=-1), dev(dzl=1), dev(dcore=1)

    copies = []
    numbers = iter(range(COPIES))

    def make(src, dst, i, to):
        return pltpu.make_async_remote_copy(
            src_ref=src, dst_ref=dst, send_sem=ssem.at[i], recv_sem=rsem.at[i],
            device_id=to, device_id_type=MESH,
        )

    def rcopy(src, dst, to):
        c = make(src, dst, next(numbers), to)
        copies.append(c)
        return c

    def start(pair):
        for c in pair:
            c.start()

    def arrived(pair):
        for c in pair:
            c.wait_recv()

    def live(k, c):
        return k < count_ref[c]

    def slot(k, c):
        return jnp.where(live(k, c), index_ref[c, k], 0)

    def mask(k, c):
        return jnp.where(live(k, c), 1.0, 0.0).astype(F32)

    def loop(f, first, last, unroll=1):
        def step(c, _):
            f(c)
            return 0

        lax.fori_loop(first, last, step, 0, unroll=unroll)

    def raw(k):
        return wg.at[k // 8, lax.rem(k, 8), :, pl.ds(0, BLK), :]

    def in_load(k):
        return pltpu.make_async_copy(w_in_ref.at[k], raw(k), load_sem.at[k])

    def out_load(k):
        return pltpu.make_async_copy(w_out_ref.at[k], w_outz.at[k], load_sem.at[SLOTS + k])

    barrier = pltpu.get_barrier_semaphore()
    peers = (zp, zm, yp, ym, xp, xm, other_zl, other_core)
    for p in peers:
        pl.semaphore_signal(barrier, inc=1, device_id=p, device_id_type=MESH)

    for b in range(DB):
        cols = pl.ds(b * BLK, BLK)
        both = jnp.concatenate(
            [tok_ref[:, cols].astype(F32), cot_ref[:, cols].astype(F32)], axis=0
        )
        x0[0, b] = both.astype(BF16)
    pl.semaphore_wait(barrier, len(peers))

    lo, hi = pl.ds(0, HALF), pl.ds(HALF, HALF)
    whole = pl.ds(0, DB)

    def shard(j, r, blocks=whole):
        g, i = PLACE[(j, r)]
        return X[g].at[i, blocks]

    def part(j, r, blocks=whole):
        return parts.at[ORDER[(j, r)], blocks]

    z_first = (
        rcopy(shard(0, 0, lo), shard(1, 0, lo), zp),
        rcopy(shard(0, 0, hi), shard(2, 0, hi), zm),
    )
    z_second = (
        rcopy(shard(0, 0, hi), shard(1, 0, hi), zp),
        rcopy(shard(0, 0, lo), shard(2, 0, lo), zm),
    )
    z_relay = (
        rcopy(shard(1, 0, lo), shard(3, 0, lo), zp),
        rcopy(shard(2, 0, hi), shard(3, 0, hi), zm),
    )
    z_cross = (
        rcopy(shard(0, 3), shard(1, 3), zp),
        rcopy(shard(0, 3), shard(2, 3), zm),
    )

    def both_ways(j, blocks):
        return (
            rcopy(shard(j, 0, blocks), shard(j, 1, blocks), yp),
            rcopy(shard(j, 0, blocks), shard(j, 2, blocks), ym),
        )

    def y_relay_of(j):
        return (
            rcopy(shard(j, 1, lo), shard(j, 3, lo), yp),
            rcopy(shard(j, 2, hi), shard(j, 3, hi), ym),
        )

    y_own = both_ways(0, whole)
    y_one = (both_ways(1, lo), both_ways(1, hi))
    y_two = (both_ways(2, hi), both_ways(2, lo))
    y_far = (both_ways(3, lo), both_ways(3, hi))
    y_relay_own = y_relay_of(0)
    y_relay_far = y_relay_of(3)

    def prepare(k):
        in_load(k).wait()
        out_load(k).wait()
        for c in range(COLS):
            m = mask(k, c)
            wi = (wg[k // 8, lax.rem(k, 8), c, :BLK, :].astype(F32) * m).astype(BF16)
            wo = (w_outz[k, c].astype(F32) * m).astype(BF16)
            w_outz[k, c] = wo
            w_inz[k, c] = wi.T
            w_fwd[c, pl.ds(k * BLK, BLK), :] = jnp.concatenate([wi, wo.T], axis=1)

    def invert(c):
        joined = [jnp.where(live(k, c), index_ref[c, k], -1) for k in range(SLOTS)]

        def one(b):
            found = jnp.int32(SLOTS)
            for k in range(SLOTS):
                found = jnp.where(joined[k] == b, k, found)
            inverse[c, b] = found

        loop(one, 0, DB)

    def forward(g):
        n = len(GROUPS[g])

        def one(c):
            lhs = jnp.concatenate(
                [X[g][:, slot(k, c)].reshape(n * PAIR, BLK) for k in range(SLOTS)], axis=1
            )
            acc = jnp.dot(lhs, w_fwd[c], preferred_element_type=F32)
            acc = acc.reshape(n, PAIR, 2 * BLK)
            pre = acc[:, :ROWS, :BLK]
            hidden_grad = acc[:, ROWS:, BLK:]
            activated, slope = gelu_parts(pre)
            pre_grad = hidden_grad * slope
            rows = pl.ds(FIRST[g] * ROWS, n * ROWS)
            hid[c, rows, :] = activated.reshape(n * ROWS, BLK).astype(BF16)
            pgr[c, rows, :] = pre_grad.reshape(n * ROWS, BLK).astype(BF16)
            zero = jnp.zeros_like(pre)
            both = jnp.concatenate(
                [
                    jnp.concatenate([pre_grad, zero], axis=2),
                    jnp.concatenate([zero, activated], axis=2),
                ],
                axis=1,
            )
            gmat[c, pl.ds(FIRST[g] * PAIR, n * PAIR), :] = both.reshape(n * PAIR, 2 * BLK).astype(BF16)

        loop(one, 0, COLS, 4)

    def spread(first, count, q_first=0, q_last=DB // 2):
        rows = pl.ds(first * ROWS, count * ROWS)

        def one(q):
            def placed(source):
                return jnp.concatenate(
                    [
                        jnp.concatenate(
                            [source[inverse[c, 2 * q], c], source[inverse[c, 2 * q + 1], c]],
                            axis=1,
                        )
                        for c in range(COLS)
                    ],
                    axis=0,
                )

            h = jnp.concatenate([hid[c, rows, :] for c in range(COLS)], axis=1)
            g = jnp.concatenate([pgr[c, rows, :] for c in range(COLS)], axis=1)
            m = jnp.dot(h, placed(w_outz), preferred_element_type=F32)
            t = jnp.dot(g, placed(w_inz), preferred_element_type=F32)
            both = jnp.concatenate(
                [m.reshape(count, ROWS, 2 * BLK), t.reshape(count, ROWS, 2 * BLK)], axis=1
            ).astype(BF16)
            for i in range(2):
                parts[pl.ds(first, count), 2 * q + i] = both[:, :, i * BLK : (i + 1) * BLK]

        loop(one, q_first, q_last, 8)

    start(z_first)
    start(y_own)
    for k in range(SLOTS):
        in_load(k).start()
        out_load(k).start()
    w_outz[SLOTS] = jnp.zeros(w_outz.shape[1:], BF16)
    w_inz[SLOTS] = jnp.zeros(w_inz.shape[1:], BF16)
    loop(prepare, 0, SLOTS // 2)
    arrived(z_first)
    start(z_second)
    start(z_relay)
    arrived(y_own)
    start(y_relay_own)
    start(y_one[0])
    start(y_two[0])
    loop(prepare, SLOTS // 2, SLOTS)
    arrived(z_second)
    start(y_one[1])
    start(y_two[1])
    loop(invert, 0, COLS)
    arrived(y_relay_own)
    forward(0)
    arrived(z_relay)
    start(z_cross)
    start(y_far[0])
    start(y_far[1])
    for pair in (*y_one, *y_two):
        arrived(pair)
    forward(1)
    spread(0, 10, 0, DB // 4)
    y_far[0][0].wait_recv()
    y_relay_far[0].start()
    y_far[1][1].wait_recv()
    y_relay_far[1].start()
    spread(0, 10, DB // 4, DB // 2)

    def add_blocks(dst, src, first, count, other=None):
        def step(i):
            at = pl.ds(first + i * 8, 8)
            frm = pl.ds(i * 8, 8)
            n = ORDER[dst]
            if other is None:
                parts[n, at] = parts[n, at] + src[frm]
            else:
                total = parts[n, at].astype(F32) + src[frm].astype(F32) + other[frm].astype(F32)
                parts[n, at] = total.astype(BF16)

        loop(step, 0, count // 8)

    oz_cross = (
        rcopy(part(1, 3, hi), zq1.at[lo], zm),
        rcopy(part(2, 3, lo), zq2.at[lo], zp),
    )
    oy_half = {
        j: (
            rcopy(part(j, 3, lo), ya.at[n], ym),
            rcopy(part(j, 3, hi), yb.at[n], yp),
        )
        for n, j in enumerate((0, 3))
    }
    oy_side = (
        rcopy(part(1, 3, lo), ya.at[2], ym),
        rcopy(part(2, 3, hi), yb.at[2], yp),
    )
    oy_full = {
        j: (
            rcopy(part(j, 1), yf1.at[j], ym),
            rcopy(part(j, 2), yf2.at[j], yp),
        )
        for j in (0,)
    }
    oy_far = tuple(
        (
            rcopy(part(3, 1, blocks), yf1.at[3, blocks], ym),
            rcopy(part(3, 2, blocks), yf2.at[3, blocks], yp),
        )
        for blocks in (lo, hi)
    )
    oy_early = (
        rcopy(part(2, 1), yf1.at[2], ym),
        rcopy(part(1, 2), yf2.at[1], yp),
    )
    oy_next = (
        rcopy(part(1, 1, hi), yf1.at[1, hi], ym),
        rcopy(part(2, 2, lo), yf2.at[2, lo], yp),
    )
    oy_last = (
        rcopy(part(1, 1, lo), yf1.at[1, lo], ym),
        rcopy(part(2, 2, hi), yf2.at[2, hi], yp),
    )
    oz_half = (
        rcopy(part(3, 0, lo), za.at[lo], zm),
        rcopy(part(3, 0, hi), zb.at[lo], zp),
    )
    oz_full = (
        rcopy(part(1, 0), zf1.at[whole], zm),
        rcopy(part(2, 0), zf2.at[whole], zp),
    )

    def y_end(j, first=0, count=DB):
        at = pl.ds(first, count)
        add_blocks((j, 0), yf1.at[j, at], first, count, yf2.at[j, at])

    start(oy_early)
    arrived(z_cross)
    y_far[0][1].wait_recv()
    y_far[1][0].wait_recv()
    arrived(y_relay_far)
    forward(2)
    spread(10, 6, 0, DB // 4)
    oy_half[3][0].start()
    oz_cross[1].start()
    spread(10, 6, DB // 4, DB // 2)
    oy_half[3][1].start()
    oz_cross[0].start()

    steps = (0, 3, 1, 2)
    base = len(copies)
    CORE, XH1, XH2, XF1, XF2, ZLO = (base + 8 * i for i in range(6))

    def core_copy(c):
        return make(wg.at[1, c], core_in.at[c], CORE + c, other_core)

    def x_half(c):
        return (
            make(wg.at[0, c, 6], xa.at[c], XH1 + c, xm),
            make(wg.at[0, c, 7], xb.at[c], XH2 + c, xp),
        )

    def x_full(c):
        return (
            make(wg.at[0, c, pl.ds(2, 2)], xf1.at[c], XF1 + c, xm),
            make(wg.at[0, c, pl.ds(4, 2)], xf2.at[c], XF2 + c, xp),
        )

    def z_low(c):
        return make(wg.at[0, c, 1], zr.at[c], ZLO + c, other_zl)

    def add_core(c):
        core_copy(c).wait_recv()
        for i in (6, 7, 2, 3, 4, 5, 0, 1):
            wg[0, c, i] = wg[0, c, i] + core_in[c, i]
        start(x_half(c))

    def add_x_half(c):
        arrived(x_half(c))
        wg[0, c, 2] = wg[0, c, 2] + xa[c]
        wg[0, c, 5] = wg[0, c, 5] + xb[c]
        start(x_full(c))

    def add_x_full(c):
        arrived(x_full(c))
        wg[0, c, 1] = (
            wg[0, c, 1].astype(F32) + xf1[c, 1].astype(F32) + xf2[c, 1].astype(F32)
        ).astype(BF16)
        z_low(c).start()

    def finish(c):
        z_low(c).wait_recv()
        total = (
            wg[0, c, 0].astype(F32) + xf1[c, 0].astype(F32) + xf2[c, 0].astype(F32)
            + zr[c].astype(F32)
        )
        igrad_ref[0, c] = total[:BLK].T
        ograd_ref[0, c] = total[BLK:]

    def weight_grad(c):
        left = gmat[c].T
        for rc in (1, 0):
            for rx in range(4):
                tiles, masks = [], []
                for rz in range(2):
                    k = (
                        lax.rem(x + steps[rx], 4) * 4
                        + lax.rem(zl + rz, 2) * 2
                        + lax.rem(core + rc, 2)
                    )
                    b = slot(k, c)
                    tiles.append(
                        jnp.concatenate(
                            [X[g][:, b].reshape(len(GROUPS[g]) * PAIR, BLK) for g in range(3)], axis=0
                        )
                    )
                    masks.append(mask(k, c) * grad_scale)
                res = jnp.dot(left, jnp.concatenate(tiles, axis=1), preferred_element_type=F32)
                for rz in range(2):
                    wg[rc, c, rx * 2 + rz] = (
                        res[:, rz * BLK : (rz + 1) * BLK] * masks[rz]
                    ).astype(BF16)
            if rc == 1:
                core_copy(c).start()

        @pl.when(c >= 1)
        def _():
            add_core(c - 1)

        @pl.when(c == 3)
        def _():
            oy_half[3][0].wait_recv()
            add_blocks((3, 1), ya.at[1], 0, HALF)
            oy_half[3][1].wait_recv()
            add_blocks((3, 2), yb.at[1], HALF, HALF)
            start(oy_far[0])

        @pl.when(c >= 4)
        def _():
            add_x_half(c - 4)

        @pl.when(c == 5)
        def _():
            start(oy_far[1])

        @pl.when(c == 7)
        def _():
            arrived(oy_far[0])
            y_end(3, 0, HALF)
            oz_half[0].start()

    loop(weight_grad, 0, COLS)
    add_core(COLS - 1)
    start(oy_side)
    start(oy_next)
    arrived(oz_cross)
    add_blocks((0, 3), zq1, HALF, HALF)
    add_blocks((0, 3), zq2, 0, HALF)
    arrived(oy_far[1])
    y_end(3, HALF, HALF)
    oz_half[1].start()
    loop(add_x_half, 4, COLS)
    loop(add_x_full, 0, 2)
    oy_side[0].wait_recv()
    add_blocks((1, 1), ya.at[2], 0, HALF)
    oy_last[0].start()
    oy_side[1].wait_recv()
    add_blocks((2, 2), yb.at[2], HALF, HALF)
    oy_last[1].start()
    start(oy_half[0])
    oz_half[0].wait_recv()
    add_blocks((1, 0), za, 0, HALF)
    loop(add_x_full, 2, 4)
    arrived(oy_early)
    arrived(oy_next)
    arrived(oy_last)
    y_end(1)
    oz_full[0].start()
    y_end(2)
    oz_half[1].wait_recv()
    add_blocks((2, 0), zb, HALF, HALF)
    oz_full[1].start()
    oy_half[0][0].wait_recv()
    add_blocks((0, 1), ya.at[0], 0, HALF)
    oy_full[0][0].start()
    oy_half[0][1].wait_recv()
    add_blocks((0, 2), yb.at[0], HALF, HALF)
    oy_full[0][1].start()
    loop(add_x_full, 4, COLS)
    loop(finish, 0, 4)
    arrived(oy_full[0])
    y_end(0)
    loop(finish, 4, COLS)
    arrived(oz_full)
    for b in range(DB):
        total = parts[0, b].astype(F32) + zf1[b].astype(F32) + zf2[b].astype(F32)
        cols = pl.ds(b * BLK, BLK)
        mixed_ref[:, cols] = total[:ROWS].astype(BF16)
        tgrad_ref[:, cols] = total[ROWS:].astype(BF16)

    for c in copies:
        c.wait_send()

    def sent(c):
        core_copy(c).wait_send()
        for r in (*x_half(c), *x_full(c)):
            r.wait_send()
        z_low(c).wait_send()

    loop(sent, 0, COLS)


def hand_on(*refs):
    n = len(refs) // 2
    for i in range(n):
        refs[n + i][...] = refs[i][...]


def body(tokens, cotangent, w_in, w_out, block_index, live_count):
    grad_scale = 1.0 / math.sqrt(tokens.shape[0] * lax.axis_size("hid") * lax.axis_size("dp"))
    vmem = pl.BlockSpec(memory_space=pltpu.VMEM)
    smem = pl.BlockSpec(memory_space=pltpu.SMEM)
    hbm = pl.BlockSpec(memory_space=pl.ANY)
    half = (HALF, PAIR, BLK)
    full = (DB, PAIR, BLK)
    tile = (2 * BLK, BLK)
    shapes = (
        jax.ShapeDtypeStruct(tokens.shape, BF16),
        jax.ShapeDtypeStruct(tokens.shape, BF16),
        jax.ShapeDtypeStruct((1, COLS, BLK, BLK), F32),
        jax.ShapeDtypeStruct((1, COLS, BLK, BLK), F32),
    )
    results = pl.pallas_call(
        functools.partial(kernel, grad_scale),
        out_shape=shapes,
        in_specs=[smem, smem, vmem, vmem, hbm, hbm],
        out_specs=(vmem, vmem, vmem, vmem),
        scratch_shapes=[
            *[pltpu.VMEM((len(g), *full), BF16) for g in GROUPS],
            pltpu.VMEM((16, *full), BF16),
            pltpu.VMEM((COLS, SLOTS * BLK, 2 * BLK), BF16),
            pltpu.VMEM((SLOTS + 1, COLS, BLK, BLK), BF16),
            pltpu.VMEM((SLOTS + 1, COLS, BLK, BLK), BF16),
            pltpu.VMEM((COLS, 16 * ROWS, BLK), BF16),
            pltpu.VMEM((COLS, 16 * ROWS, BLK), BF16),
            pltpu.VMEM((COLS, 16 * PAIR, 2 * BLK), BF16),
            pltpu.VMEM((2, COLS, 8, *tile), BF16),
            pltpu.VMEM((COLS, 8, *tile), BF16),
            pltpu.VMEM((COLS, *tile), BF16),
            pltpu.VMEM((COLS, *tile), BF16),
            pltpu.VMEM((COLS, 2, *tile), BF16),
            pltpu.VMEM((COLS, 2, *tile), BF16),
            pltpu.VMEM((COLS, *tile), BF16),
            pltpu.VMEM((3, *half), BF16),
            pltpu.VMEM((3, *half), BF16),
            pltpu.VMEM((4, *full), BF16),
            pltpu.VMEM((4, *full), BF16),
            pltpu.VMEM(half, BF16),
            pltpu.VMEM(half, BF16),
            *[pltpu.VMEM(full, BF16) for _ in range(2)],
            *[pltpu.VMEM(half, BF16) for _ in range(2)],
            pltpu.SMEM((COLS, DB), jnp.int32),
            pltpu.SemaphoreType.DMA((2 * SLOTS,)),
            pltpu.SemaphoreType.DMA((COPIES,)),
            pltpu.SemaphoreType.DMA((COPIES,)),
        ],
        compiler_params=pltpu.CompilerParams(
            collective_id=0, has_side_effects=True, vmem_limit_bytes=62 * 2**20
        ),
        cost_estimate=pl.CostEstimate(
            flops=3 * 2 * 2 * 384 * 2048 * 1024, bytes_accessed=12 * 2**20, transcendentals=384 * 1024
        ),
    )(block_index.T, live_count, tokens, cotangent, w_in, w_out)
    return pl.pallas_call(
        hand_on,
        out_shape=shapes,
        in_specs=[vmem] * len(shapes),
        out_specs=(vmem,) * len(shapes),
    )(*results)


def solution(mesh):
    in_specs = (
        P(("dp", "hid"), None),
        P(("dp", "hid"), None),
        P(None, "hid", None, None),
        P(None, "hid", None, None),
        P(None, "hid"),
        P("hid"),
    )
    out_specs = (
        P(("dp", "hid"), None),
        P(("dp", "hid"), None),
        P("dp", "hid", None, None),
        P("dp", "hid", None, None),
    )
    return jax.shard_map(body, mesh=mesh, in_specs=in_specs, out_specs=out_specs, check_vma=False)
```

```python
import functools
import math

import jax
import jax.numpy as jnp
from jax import lax
from jax.experimental import pallas as pl
from jax.experimental.pallas import tpu as pltpu
from jax.sharding import PartitionSpec as P

MESH = pl.DeviceIdType.MESH
gelu_root = 0.7978845608028654
gelu_cubic = 0.044715

BLK = 128
DB = 32
SLOTS = 16
COLS = 8
ROWS = 24
PAIR = 2 * ROWS
HALF = DB // 2
F32 = jnp.float32
BF16 = jnp.bfloat16

GROUPS = (
    ((0, 0), (0, 1), (0, 2), (0, 3)),
    ((1, 0), (1, 1), (1, 2), (2, 0), (2, 1), (2, 2)),
    ((3, 0), (3, 1), (3, 2), (3, 3), (1, 3), (2, 3)),
)
PLACE = {jr: (g, i) for g, group in enumerate(GROUPS) for i, jr in enumerate(group)}
ORDER = {jr: n for n, jr in enumerate(jr for group in GROUPS for jr in group)}
FIRST = (0, 4, 10)
COPIES = 120


def gelu_parts(pre):
    argument = gelu_root * (pre + gelu_cubic * pre * pre * pre)
    tangent = jnp.tanh(argument)
    activated = 0.5 * pre * (1.0 + tangent)
    slope = 0.5 * (1.0 + tangent) + 0.5 * pre * (1.0 - tangent * tangent) * gelu_root * (
        1.0 + 3.0 * gelu_cubic * pre * pre
    )
    return (activated, slope)


def kernel(
    grad_scale,
    index_ref, count_ref,
    tok_ref, cot_ref, w_in_ref, w_out_ref,
    mixed_ref, tgrad_ref, igrad_ref, ograd_ref,
    x0, x1, x2, parts,
    w_fwd, w_outz, w_inz,
    hid, pgr, gmat,
    wg, core_in, xa, xb, xf1, xf2, zr,
    ya, yb, yf1, yf2, za, zb, zf1, zf2, zq1, zq2,
    inverse,
    load_sem, ssem, rsem,
):
    X = (x0, x1, x2)
    dp = lax.axis_index("dp")
    hd = lax.axis_index("hid")
    x, zl, core = dp // 4, lax.rem(dp // 2, 2), lax.rem(dp, 2)
    y, zh = hd // 4, lax.rem(hd, 4)

    def dev(dx=0, dzl=0, dcore=0, dy=0, dzh=0):
        return (
            lax.rem(x + dx + 4, 4) * 4 + lax.rem(zl + dzl, 2) * 2 + lax.rem(core + dcore, 2),
            lax.rem(y + dy + 4, 4) * 4 + lax.rem(zh + dzh + 4, 4),
        )

    zp, zm, yp, ym = dev(dzh=1), dev(dzh=-1), dev(dy=1), dev(dy=-1)
    xp, xm, other_zl, other_core = dev(dx=1), dev(dx=-1), dev(dzl=1), dev(dcore=1)

    copies = []
    numbers = iter(range(COPIES))

    def make(src, dst, i, to):
        return pltpu.make_async_remote_copy(
            src_ref=src, dst_ref=dst, send_sem=ssem.at[i], recv_sem=rsem.at[i],
            device_id=to, device_id_type=MESH,
        )

    def rcopy(src, dst, to):
        c = make(src, dst, next(numbers), to)
        copies.append(c)
        return c

    def start(pair):
        for c in pair:
            c.start()

    def arrived(pair):
        for c in pair:
            c.wait_recv()

    def live(k, c):
        return k < count_ref[c]

    def slot(k, c):
        return jnp.where(live(k, c), index_ref[c, k], 0)

    def mask(k, c):
        return jnp.where(live(k, c), 1.0, 0.0).astype(F32)

    def loop(f, first, last, unroll=1):
        def step(c, _):
            f(c)
            return 0

        lax.fori_loop(first, last, step, 0, unroll=unroll)

    def raw(k):
        return wg.at[k // 8, lax.rem(k, 8), :, pl.ds(0, BLK), :]

    def in_load(k):
        return pltpu.make_async_copy(w_in_ref.at[k], raw(k), load_sem.at[k])

    def out_load(k):
        return pltpu.make_async_copy(w_out_ref.at[k], w_outz.at[k], load_sem.at[SLOTS + k])

    barrier = pltpu.get_barrier_semaphore()
    peers = (zp, zm, yp, ym, xp, xm, other_zl, other_core)
    for p in peers:
        pl.semaphore_signal(barrier, inc=1, device_id=p, device_id_type=MESH)

    for b in range(DB):
        cols = pl.ds(b * BLK, BLK)
        both = jnp.concatenate(
            [tok_ref[:, cols].astype(F32), cot_ref[:, cols].astype(F32)], axis=0
        )
        x0[0, b] = both.astype(BF16)
    pl.semaphore_wait(barrier, len(peers))

    lo, hi = pl.ds(0, HALF), pl.ds(HALF, HALF)
    whole = pl.ds(0, DB)

    def shard(j, r, blocks=whole):
        g, i = PLACE[(j, r)]
        return X[g].at[i, blocks]

    def part(j, r, blocks=whole):
        return parts.at[ORDER[(j, r)], blocks]

    z_first = (
        rcopy(shard(0, 0, lo), shard(1, 0, lo), zp),
        rcopy(shard(0, 0, hi), shard(2, 0, hi), zm),
    )
    z_second = (
        rcopy(shard(0, 0, hi), shard(1, 0, hi), zp),
        rcopy(shard(0, 0, lo), shard(2, 0, lo), zm),
    )
    z_relay = (
        rcopy(shard(1, 0, lo), shard(3, 0, lo), zp),
        rcopy(shard(2, 0, hi), shard(3, 0, hi), zm),
    )
    z_cross = (
        rcopy(shard(0, 3), shard(1, 3), zp),
        rcopy(shard(0, 3), shard(2, 3), zm),
    )

    def both_ways(j, blocks):
        return (
            rcopy(shard(j, 0, blocks), shard(j, 1, blocks), yp),
            rcopy(shard(j, 0, blocks), shard(j, 2, blocks), ym),
        )

    def y_relay_of(j):
        return (
            rcopy(shard(j, 1, lo), shard(j, 3, lo), yp),
            rcopy(shard(j, 2, hi), shard(j, 3, hi), ym),
        )

    y_own = both_ways(0, whole)
    y_one = (both_ways(1, lo), both_ways(1, hi))
    y_two = (both_ways(2, hi), both_ways(2, lo))
    y_far = (both_ways(3, lo), both_ways(3, hi))
    y_relay_own = y_relay_of(0)
    y_relay_far = y_relay_of(3)

    def prepare(k):
        in_load(k).wait()
        out_load(k).wait()
        for c in range(COLS):
            m = mask(k, c)
            wi = (wg[k // 8, lax.rem(k, 8), c, :BLK, :].astype(F32) * m).astype(BF16)
            wo = (w_outz[k, c].astype(F32) * m).astype(BF16)
            w_outz[k, c] = wo
            w_inz[k, c] = wi.T
            w_fwd[c, pl.ds(k * BLK, BLK), :] = jnp.concatenate([wi, wo.T], axis=1)

    def invert(c):
        joined = [jnp.where(live(k, c), index_ref[c, k], -1) for k in range(SLOTS)]

        def one(b):
            found = jnp.int32(SLOTS)
            for k in range(SLOTS):
                found = jnp.where(joined[k] == b, k, found)
            inverse[c, b] = found

        loop(one, 0, DB)

    def forward(g):
        n = len(GROUPS[g])

        def one(c):
            lhs = jnp.concatenate(
                [X[g][:, slot(k, c)].reshape(n * PAIR, BLK) for k in range(SLOTS)], axis=1
            )
            acc = jnp.dot(lhs, w_fwd[c], preferred_element_type=F32)
            acc = acc.reshape(n, PAIR, 2 * BLK)
            pre = acc[:, :ROWS, :BLK]
            hidden_grad = acc[:, ROWS:, BLK:]
            activated, slope = gelu_parts(pre)
            pre_grad = hidden_grad * slope
            rows = pl.ds(FIRST[g] * ROWS, n * ROWS)
            hid[c, rows, :] = activated.reshape(n * ROWS, BLK).astype(BF16)
            pgr[c, rows, :] = pre_grad.reshape(n * ROWS, BLK).astype(BF16)
            zero = jnp.zeros_like(pre)
            both = jnp.concatenate(
                [
                    jnp.concatenate([pre_grad, zero], axis=2),
                    jnp.concatenate([zero, activated], axis=2),
                ],
                axis=1,
            )
            gmat[c, pl.ds(FIRST[g] * PAIR, n * PAIR), :] = both.reshape(n * PAIR, 2 * BLK).astype(BF16)

        loop(one, 0, COLS, 4)

    def spread(first, count, q_first=0, q_last=DB // 2):
        rows = pl.ds(first * ROWS, count * ROWS)

        def one(q):
            def placed(source):
                return jnp.concatenate(
                    [
                        jnp.concatenate(
                            [source[inverse[c, 2 * q], c], source[inverse[c, 2 * q + 1], c]],
                            axis=1,
                        )
                        for c in range(COLS)
                    ],
                    axis=0,
                )

            h = jnp.concatenate([hid[c, rows, :] for c in range(COLS)], axis=1)
            g = jnp.concatenate([pgr[c, rows, :] for c in range(COLS)], axis=1)
            m = jnp.dot(h, placed(w_outz), preferred_element_type=F32)
            t = jnp.dot(g, placed(w_inz), preferred_element_type=F32)
            both = jnp.concatenate(
                [m.reshape(count, ROWS, 2 * BLK), t.reshape(count, ROWS, 2 * BLK)], axis=1
            ).astype(BF16)
            for i in range(2):
                parts[pl.ds(first, count), 2 * q + i] = both[:, :, i * BLK : (i + 1) * BLK]

        loop(one, q_first, q_last, 8)

    start(z_first)
    start(y_own)
    for k in range(SLOTS):
        in_load(k).start()
        out_load(k).start()
    w_outz[SLOTS] = jnp.zeros(w_outz.shape[1:], BF16)
    w_inz[SLOTS] = jnp.zeros(w_inz.shape[1:], BF16)
    loop(prepare, 0, SLOTS // 2)
    arrived(z_first)
    start(z_second)
    start(z_relay)
    arrived(y_own)
    start(y_relay_own)
    start(y_one[0])
    start(y_two[0])
    loop(prepare, SLOTS // 2, SLOTS)
    arrived(z_second)
    start(y_one[1])
    start(y_two[1])
    loop(invert, 0, COLS)
    arrived(y_relay_own)
    forward(0)
    arrived(z_relay)
    start(z_cross)
    start(y_far[0])
    start(y_far[1])
    for pair in (*y_one, *y_two):
        arrived(pair)
    forward(1)
    spread(0, 10, 0, DB // 4)
    y_far[0][0].wait_recv()
    y_relay_far[0].start()
    y_far[1][1].wait_recv()
    y_relay_far[1].start()
    spread(0, 10, DB // 4, DB // 2)

    def add_blocks(dst, src, first, count, other=None):
        def step(i):
            at = pl.ds(first + i * 8, 8)
            frm = pl.ds(i * 8, 8)
            n = ORDER[dst]
            if other is None:
                parts[n, at] = parts[n, at] + src[frm]
            else:
                total = parts[n, at].astype(F32) + src[frm].astype(F32) + other[frm].astype(F32)
                parts[n, at] = total.astype(BF16)

        loop(step, 0, count // 8)

    oz_cross = (
        rcopy(part(1, 3, hi), zq1.at[lo], zm),
        rcopy(part(2, 3, lo), zq2.at[lo], zp),
    )
    oy_half = {
        j: (
            rcopy(part(j, 3, lo), ya.at[n], ym),
            rcopy(part(j, 3, hi), yb.at[n], yp),
        )
        for n, j in enumerate((0, 3))
    }
    oy_side = (
        rcopy(part(1, 3, lo), ya.at[2], ym),
        rcopy(part(2, 3, hi), yb.at[2], yp),
    )
    oy_full = {
        j: (
            rcopy(part(j, 1), yf1.at[j], ym),
            rcopy(part(j, 2), yf2.at[j], yp),
        )
        for j in (0,)
    }
    oy_far = tuple(
        (
            rcopy(part(3, 1, blocks), yf1.at[3, blocks], ym),
            rcopy(part(3, 2, blocks), yf2.at[3, blocks], yp),
        )
        for blocks in (lo, hi)
    )
    oy_early = (
        rcopy(part(2, 1), yf1.at[2], ym),
        rcopy(part(1, 2), yf2.at[1], yp),
    )
    oy_next = (
        rcopy(part(1, 1, hi), yf1.at[1, hi], ym),
        rcopy(part(2, 2, lo), yf2.at[2, lo], yp),
    )
    oy_last = (
        rcopy(part(1, 1, lo), yf1.at[1, lo], ym),
        rcopy(part(2, 2, hi), yf2.at[2, hi], yp),
    )
    oz_half = (
        rcopy(part(3, 0, lo), za.at[lo], zm),
        rcopy(part(3, 0, hi), zb.at[lo], zp),
    )
    oz_first = (
        rcopy(part(1, 0, hi), zf1.at[hi], zm),
        rcopy(part(2, 0, lo), zf2.at[lo], zp),
    )
    oz_second = (
        rcopy(part(1, 0, lo), zf1.at[lo], zm),
        rcopy(part(2, 0, hi), zf2.at[hi], zp),
    )

    def y_end(j, first=0, count=DB):
        at = pl.ds(first, count)
        add_blocks((j, 0), yf1.at[j, at], first, count, yf2.at[j, at])

    start(oy_early)
    arrived(z_cross)
    y_far[0][1].wait_recv()
    y_far[1][0].wait_recv()
    arrived(y_relay_far)
    forward(2)
    spread(10, 6, 0, DB // 4)
    oy_half[3][0].start()
    oz_cross[1].start()
    spread(10, 6, DB // 4, DB // 2)
    oy_half[3][1].start()
    oz_cross[0].start()

    steps = (0, 3, 1, 2)
    base = len(copies)
    CORE, XH1, XH2, XF1, XF2, ZLO = (base + 8 * i for i in range(6))

    def core_copy(c):
        return make(wg.at[1, c], core_in.at[c], CORE + c, other_core)

    def x_half(c):
        return (
            make(wg.at[0, c, 6], xa.at[c], XH1 + c, xm),
            make(wg.at[0, c, 7], xb.at[c], XH2 + c, xp),
        )

    def x_full(c):
        return (
            make(wg.at[0, c, pl.ds(2, 2)], xf1.at[c], XF1 + c, xm),
            make(wg.at[0, c, pl.ds(4, 2)], xf2.at[c], XF2 + c, xp),
        )

    def z_low(c):
        return make(wg.at[0, c, 1], zr.at[c], ZLO + c, other_zl)

    def add_core(c):
        core_copy(c).wait_recv()
        for i in (6, 7, 2, 3, 4, 5, 0, 1):
            wg[0, c, i] = wg[0, c, i] + core_in[c, i]
        start(x_half(c))

    def add_x_half(c):
        arrived(x_half(c))
        wg[0, c, 2] = wg[0, c, 2] + xa[c]
        wg[0, c, 5] = wg[0, c, 5] + xb[c]
        start(x_full(c))

    def add_x_full(c):
        arrived(x_full(c))
        wg[0, c, 1] = (
            wg[0, c, 1].astype(F32) + xf1[c, 1].astype(F32) + xf2[c, 1].astype(F32)
        ).astype(BF16)
        z_low(c).start()

    def finish(c):
        z_low(c).wait_recv()
        total = (
            wg[0, c, 0].astype(F32) + xf1[c, 0].astype(F32) + xf2[c, 0].astype(F32)
            + zr[c].astype(F32)
        )
        igrad_ref[0, c] = total[:BLK].T
        ograd_ref[0, c] = total[BLK:]

    def weight_grad(c):
        left = gmat[c].T
        for rc in (1, 0):
            for rx in range(4):
                tiles, masks = [], []
                for rz in range(2):
                    k = (
                        lax.rem(x + steps[rx], 4) * 4
                        + lax.rem(zl + rz, 2) * 2
                        + lax.rem(core + rc, 2)
                    )
                    b = slot(k, c)
                    tiles.append(
                        jnp.concatenate(
                            [X[g][:, b].reshape(len(GROUPS[g]) * PAIR, BLK) for g in range(3)], axis=0
                        )
                    )
                    masks.append(mask(k, c) * grad_scale)
                res = jnp.dot(left, jnp.concatenate(tiles, axis=1), preferred_element_type=F32)
                for rz in range(2):
                    wg[rc, c, rx * 2 + rz] = (
                        res[:, rz * BLK : (rz + 1) * BLK] * masks[rz]
                    ).astype(BF16)
            if rc == 1:
                core_copy(c).start()

        @pl.when(c >= 1)
        def _():
            add_core(c - 1)

        @pl.when(c == 3)
        def _():
            oy_half[3][0].wait_recv()
            add_blocks((3, 1), ya.at[1], 0, HALF)
            oy_half[3][1].wait_recv()
            add_blocks((3, 2), yb.at[1], HALF, HALF)
            start(oy_far[0])

        @pl.when(c >= 4)
        def _():
            add_x_half(c - 4)

        @pl.when(c == 5)
        def _():
            start(oy_far[1])

        @pl.when(c == 7)
        def _():
            arrived(oy_far[0])
            y_end(3, 0, HALF)
            oz_half[0].start()

    loop(weight_grad, 0, COLS)
    add_core(COLS - 1)
    start(oy_next)
    arrived(oz_cross)
    add_blocks((0, 3), zq1, HALF, HALF)
    add_blocks((0, 3), zq2, 0, HALF)
    arrived(oy_far[1])
    y_end(3, HALF, HALF)
    oz_half[1].start()
    start(oy_side)
    loop(add_x_half, 4, 6)
    arrived(oy_early)
    arrived(oy_next)
    y_end(1, HALF, HALF)
    oz_first[0].start()
    y_end(2, 0, HALF)
    oz_first[1].start()
    loop(add_x_half, 6, COLS)
    loop(add_x_full, 0, 1)
    oy_side[0].wait_recv()
    add_blocks((1, 1), ya.at[2], 0, HALF)
    oy_last[0].start()
    oy_side[1].wait_recv()
    add_blocks((2, 2), yb.at[2], HALF, HALF)
    oy_last[1].start()
    start(oy_half[0])
    oz_half[0].wait_recv()
    add_blocks((1, 0), za, 0, HALF)
    oz_half[1].wait_recv()
    add_blocks((2, 0), zb, HALF, HALF)
    arrived(oy_last)
    y_end(1, 0, HALF)
    oz_second[0].start()
    y_end(2, HALF, HALF)
    oz_second[1].start()
    loop(add_x_full, 1, 4)
    oy_half[0][0].wait_recv()
    add_blocks((0, 1), ya.at[0], 0, HALF)
    oy_full[0][0].start()
    oy_half[0][1].wait_recv()
    add_blocks((0, 2), yb.at[0], HALF, HALF)
    oy_full[0][1].start()
    loop(add_x_full, 4, COLS)
    loop(finish, 0, 4)
    arrived(oy_full[0])
    y_end(0)
    loop(finish, 4, COLS)
    arrived(oz_first)
    arrived(oz_second)
    for b in range(DB):
        total = parts[0, b].astype(F32) + zf1[b].astype(F32) + zf2[b].astype(F32)
        cols = pl.ds(b * BLK, BLK)
        mixed_ref[:, cols] = total[:ROWS].astype(BF16)
        tgrad_ref[:, cols] = total[ROWS:].astype(BF16)

    for c in copies:
        c.wait_send()

    def sent(c):
        core_copy(c).wait_send()
        for r in (*x_half(c), *x_full(c)):
            r.wait_send()
        z_low(c).wait_send()

    loop(sent, 0, COLS)


def hand_on(*refs):
    n = len(refs) // 2
    for i in range(n):
        refs[n + i][...] = refs[i][...]


def body(tokens, cotangent, w_in, w_out, block_index, live_count):
    grad_scale = 1.0 / math.sqrt(tokens.shape[0] * lax.axis_size("hid") * lax.axis_size("dp"))
    vmem = pl.BlockSpec(memory_space=pltpu.VMEM)
    smem = pl.BlockSpec(memory_space=pltpu.SMEM)
    hbm = pl.BlockSpec(memory_space=pl.ANY)
    half = (HALF, PAIR, BLK)
    full = (DB, PAIR, BLK)
    tile = (2 * BLK, BLK)
    shapes = (
        jax.ShapeDtypeStruct(tokens.shape, BF16),
        jax.ShapeDtypeStruct(tokens.shape, BF16),
        jax.ShapeDtypeStruct((1, COLS, BLK, BLK), F32),
        jax.ShapeDtypeStruct((1, COLS, BLK, BLK), F32),
    )
    results = pl.pallas_call(
        functools.partial(kernel, grad_scale),
        out_shape=shapes,
        in_specs=[smem, smem, vmem, vmem, hbm, hbm],
        out_specs=(vmem, vmem, vmem, vmem),
        scratch_shapes=[
            *[pltpu.VMEM((len(g), *full), BF16) for g in GROUPS],
            pltpu.VMEM((16, *full), BF16),
            pltpu.VMEM((COLS, SLOTS * BLK, 2 * BLK), BF16),
            pltpu.VMEM((SLOTS + 1, COLS, BLK, BLK), BF16),
            pltpu.VMEM((SLOTS + 1, COLS, BLK, BLK), BF16),
            pltpu.VMEM((COLS, 16 * ROWS, BLK), BF16),
            pltpu.VMEM((COLS, 16 * ROWS, BLK), BF16),
            pltpu.VMEM((COLS, 16 * PAIR, 2 * BLK), BF16),
            pltpu.VMEM((2, COLS, 8, *tile), BF16),
            pltpu.VMEM((COLS, 8, *tile), BF16),
            pltpu.VMEM((COLS, *tile), BF16),
            pltpu.VMEM((COLS, *tile), BF16),
            pltpu.VMEM((COLS, 2, *tile), BF16),
            pltpu.VMEM((COLS, 2, *tile), BF16),
            pltpu.VMEM((COLS, *tile), BF16),
            pltpu.VMEM((3, *half), BF16),
            pltpu.VMEM((3, *half), BF16),
            pltpu.VMEM((4, *full), BF16),
            pltpu.VMEM((4, *full), BF16),
            pltpu.VMEM(half, BF16),
            pltpu.VMEM(half, BF16),
            *[pltpu.VMEM(full, BF16) for _ in range(2)],
            *[pltpu.VMEM(half, BF16) for _ in range(2)],
            pltpu.SMEM((COLS, DB), jnp.int32),
            pltpu.SemaphoreType.DMA((2 * SLOTS,)),
            pltpu.SemaphoreType.DMA((COPIES,)),
            pltpu.SemaphoreType.DMA((COPIES,)),
        ],
        compiler_params=pltpu.CompilerParams(
            collective_id=0, has_side_effects=True, vmem_limit_bytes=62 * 2**20
        ),
        cost_estimate=pl.CostEstimate(
            flops=3 * 2 * 2 * 384 * 2048 * 1024, bytes_accessed=12 * 2**20, transcendentals=384 * 1024
        ),
    )(block_index.T, live_count, tokens, cotangent, w_in, w_out)
    return pl.pallas_call(
        hand_on,
        out_shape=shapes,
        in_specs=[vmem] * len(shapes),
        out_specs=(vmem,) * len(shapes),
    )(*results)


def solution(mesh):
    in_specs = (
        P(("dp", "hid"), None),
        P(("dp", "hid"), None),
        P(None, "hid", None, None),
        P(None, "hid", None, None),
        P(None, "hid"),
        P("hid"),
    )
    out_specs = (
        P(("dp", "hid"), None),
        P(("dp", "hid"), None),
        P("dp", "hid", None, None),
        P("dp", "hid", None, None),
    )
    return jax.shard_map(body, mesh=mesh, in_specs=in_specs, out_specs=out_specs, check_vma=False)
```

```python
import functools
import math

import jax
import jax.numpy as jnp
from jax import lax
from jax.experimental import pallas as pl
from jax.experimental.pallas import tpu as pltpu
from jax.sharding import PartitionSpec as P

MESH = pl.DeviceIdType.MESH
gelu_root = 0.7978845608028654
gelu_cubic = 0.044715

BLK = 128
DB = 32
SLOTS = 16
COLS = 8
ROWS = 24
PAIR = 2 * ROWS
HALF = DB // 2
F32 = jnp.float32
BF16 = jnp.bfloat16

GROUPS = (
    ((0, 0), (0, 1), (0, 2), (0, 3)),
    ((1, 0), (1, 1), (1, 2), (2, 0), (2, 1), (2, 2)),
    ((3, 0), (3, 1), (3, 2), (3, 3), (1, 3), (2, 3)),
)
PLACE = {jr: (g, i) for g, group in enumerate(GROUPS) for i, jr in enumerate(group)}
ORDER = {jr: n for n, jr in enumerate(jr for group in GROUPS for jr in group)}
FIRST = (0, 4, 10)
COPIES = 120


def gelu_parts(pre):
    argument = gelu_root * (pre + gelu_cubic * pre * pre * pre)
    tangent = jnp.tanh(argument)
    activated = 0.5 * pre * (1.0 + tangent)
    slope = 0.5 * (1.0 + tangent) + 0.5 * pre * (1.0 - tangent * tangent) * gelu_root * (
        1.0 + 3.0 * gelu_cubic * pre * pre
    )
    return (activated, slope)


def kernel(
    grad_scale,
    index_ref, count_ref,
    tok_ref, cot_ref, w_in_ref, w_out_ref,
    mixed_ref, tgrad_ref, igrad_ref, ograd_ref,
    x0, x1, x2, parts,
    w_fwd, w_outz, w_inz,
    hid, pgr, gmat,
    wg, core_in, xa, xb, xf1, xf2, zr,
    ya, yb, yf1, yf2, za, zb, zf1, zf2, zq1, zq2,
    inverse,
    load_sem, ssem, rsem,
):
    X = (x0, x1, x2)
    dp = lax.axis_index("dp")
    hd = lax.axis_index("hid")
    x, zl, core = dp // 4, lax.rem(dp // 2, 2), lax.rem(dp, 2)
    y, zh = hd // 4, lax.rem(hd, 4)

    def dev(dx=0, dzl=0, dcore=0, dy=0, dzh=0):
        return (
            lax.rem(x + dx + 4, 4) * 4 + lax.rem(zl + dzl, 2) * 2 + lax.rem(core + dcore, 2),
            lax.rem(y + dy + 4, 4) * 4 + lax.rem(zh + dzh + 4, 4),
        )

    zp, zm, yp, ym = dev(dzh=1), dev(dzh=-1), dev(dy=1), dev(dy=-1)
    xp, xm, other_zl, other_core = dev(dx=1), dev(dx=-1), dev(dzl=1), dev(dcore=1)

    copies = []
    numbers = iter(range(COPIES))

    def make(src, dst, i, to):
        return pltpu.make_async_remote_copy(
            src_ref=src, dst_ref=dst, send_sem=ssem.at[i], recv_sem=rsem.at[i],
            device_id=to, device_id_type=MESH,
        )

    def rcopy(src, dst, to):
        c = make(src, dst, next(numbers), to)
        copies.append(c)
        return c

    def start(pair):
        for c in pair:
            c.start()

    def arrived(pair):
        for c in pair:
            c.wait_recv()

    def live(k, c):
        return k < count_ref[c]

    def slot(k, c):
        return jnp.where(live(k, c), index_ref[c, k], 0)

    def mask(k, c):
        return jnp.where(live(k, c), 1.0, 0.0).astype(F32)

    def loop(f, first, last, unroll=1):
        def step(c, _):
            f(c)
            return 0

        lax.fori_loop(first, last, step, 0, unroll=unroll)

    def raw(k):
        return wg.at[k // 8, lax.rem(k, 8), :, pl.ds(0, BLK), :]

    def in_load(k):
        return pltpu.make_async_copy(w_in_ref.at[k], raw(k), load_sem.at[k])

    def out_load(k):
        return pltpu.make_async_copy(w_out_ref.at[k], w_outz.at[k], load_sem.at[SLOTS + k])

    barrier = pltpu.get_barrier_semaphore()
    peers = (zp, zm, yp, ym, xp, xm, other_zl, other_core)
    for p in peers:
        pl.semaphore_signal(barrier, inc=1, device_id=p, device_id_type=MESH)

    for b in range(DB):
        cols = pl.ds(b * BLK, BLK)
        both = jnp.concatenate(
            [tok_ref[:, cols].astype(F32), cot_ref[:, cols].astype(F32)], axis=0
        )
        x0[0, b] = both.astype(BF16)
    pl.semaphore_wait(barrier, len(peers))

    lo, hi = pl.ds(0, HALF), pl.ds(HALF, HALF)
    whole = pl.ds(0, DB)

    def shard(j, r, blocks=whole):
        g, i = PLACE[(j, r)]
        return X[g].at[i, blocks]

    def part(j, r, blocks=whole):
        return parts.at[ORDER[(j, r)], blocks]

    z_first = (
        rcopy(shard(0, 0, lo), shard(1, 0, lo), zp),
        rcopy(shard(0, 0, hi), shard(2, 0, hi), zm),
    )
    z_second = (
        rcopy(shard(0, 0, hi), shard(1, 0, hi), zp),
        rcopy(shard(0, 0, lo), shard(2, 0, lo), zm),
    )
    z_relay = (
        rcopy(shard(1, 0, lo), shard(3, 0, lo), zp),
        rcopy(shard(2, 0, hi), shard(3, 0, hi), zm),
    )
    z_cross = (
        rcopy(shard(0, 3), shard(1, 3), zp),
        rcopy(shard(0, 3), shard(2, 3), zm),
    )

    def both_ways(j, blocks):
        return (
            rcopy(shard(j, 0, blocks), shard(j, 1, blocks), yp),
            rcopy(shard(j, 0, blocks), shard(j, 2, blocks), ym),
        )

    def y_relay_of(j):
        return (
            rcopy(shard(j, 1, lo), shard(j, 3, lo), yp),
            rcopy(shard(j, 2, hi), shard(j, 3, hi), ym),
        )

    y_own = both_ways(0, whole)
    y_one = (both_ways(1, lo), both_ways(1, hi))
    y_two = (both_ways(2, hi), both_ways(2, lo))
    y_far = (both_ways(3, lo), both_ways(3, hi))
    y_relay_own = y_relay_of(0)
    y_relay_far = y_relay_of(3)

    def prepare(k):
        in_load(k).wait()
        out_load(k).wait()
        for c in range(COLS):
            m = mask(k, c)
            wi = (wg[k // 8, lax.rem(k, 8), c, :BLK, :].astype(F32) * m).astype(BF16)
            wo = (w_outz[k, c].astype(F32) * m).astype(BF16)
            w_outz[k, c] = wo
            w_inz[k, c] = wi.T
            w_fwd[c, pl.ds(k * BLK, BLK), :] = jnp.concatenate([wi, wo.T], axis=1)

    def invert(c):
        joined = [jnp.where(live(k, c), index_ref[c, k], -1) for k in range(SLOTS)]

        def one(b):
            found = jnp.int32(SLOTS)
            for k in range(SLOTS):
                found = jnp.where(joined[k] == b, k, found)
            inverse[c, b] = found

        loop(one, 0, DB)

    def forward(g):
        n = len(GROUPS[g])

        def one(c):
            lhs = jnp.concatenate(
                [X[g][:, slot(k, c)].reshape(n * PAIR, BLK) for k in range(SLOTS)], axis=1
            )
            acc = jnp.dot(lhs, w_fwd[c], preferred_element_type=F32)
            acc = acc.reshape(n, PAIR, 2 * BLK)
            pre = acc[:, :ROWS, :BLK]
            hidden_grad = acc[:, ROWS:, BLK:]
            activated, slope = gelu_parts(pre)
            pre_grad = hidden_grad * slope
            rows = pl.ds(FIRST[g] * ROWS, n * ROWS)
            hid[c, rows, :] = activated.reshape(n * ROWS, BLK).astype(BF16)
            pgr[c, rows, :] = pre_grad.reshape(n * ROWS, BLK).astype(BF16)
            zero = jnp.zeros_like(pre)
            both = jnp.concatenate(
                [
                    jnp.concatenate([pre_grad, zero], axis=2),
                    jnp.concatenate([zero, activated], axis=2),
                ],
                axis=1,
            )
            gmat[c, pl.ds(FIRST[g] * PAIR, n * PAIR), :] = both.reshape(n * PAIR, 2 * BLK).astype(BF16)

        loop(one, 0, COLS, 4)

    def spread(first, count, q_first=0, q_last=DB // 2):
        rows = pl.ds(first * ROWS, count * ROWS)

        def one(q):
            def placed(source):
                return jnp.concatenate(
                    [
                        jnp.concatenate(
                            [source[inverse[c, 2 * q], c], source[inverse[c, 2 * q + 1], c]],
                            axis=1,
                        )
                        for c in range(COLS)
                    ],
                    axis=0,
                )

            h = jnp.concatenate([hid[c, rows, :] for c in range(COLS)], axis=1)
            g = jnp.concatenate([pgr[c, rows, :] for c in range(COLS)], axis=1)
            m = jnp.dot(h, placed(w_outz), preferred_element_type=F32)
            t = jnp.dot(g, placed(w_inz), preferred_element_type=F32)
            both = jnp.concatenate(
                [m.reshape(count, ROWS, 2 * BLK), t.reshape(count, ROWS, 2 * BLK)], axis=1
            ).astype(BF16)
            for i in range(2):
                parts[pl.ds(first, count), 2 * q + i] = both[:, :, i * BLK : (i + 1) * BLK]

        loop(one, q_first, q_last, 8)

    start(z_first)
    start(y_own)
    for k in range(SLOTS):
        in_load(k).start()
        out_load(k).start()
    w_outz[SLOTS] = jnp.zeros(w_outz.shape[1:], BF16)
    w_inz[SLOTS] = jnp.zeros(w_inz.shape[1:], BF16)
    loop(prepare, 0, SLOTS // 2)
    arrived(z_first)
    start(z_second)
    start(z_relay)
    arrived(y_own)
    start(y_relay_own)
    start(y_one[0])
    start(y_two[0])
    loop(prepare, SLOTS // 2, SLOTS)
    arrived(z_second)
    start(y_one[1])
    start(y_two[1])
    loop(invert, 0, COLS)
    arrived(y_relay_own)
    forward(0)
    arrived(z_relay)
    start(z_cross)
    start(y_far[0])
    start(y_far[1])
    for pair in (*y_one, *y_two):
        arrived(pair)
    forward(1)
    spread(0, 10, 0, DB // 4)
    y_far[0][0].wait_recv()
    y_relay_far[0].start()
    y_far[1][1].wait_recv()
    y_relay_far[1].start()
    spread(0, 10, DB // 4, DB // 2)

    def add_blocks(dst, src, first, count, other=None):
        def step(i):
            at = pl.ds(first + i * 8, 8)
            frm = pl.ds(i * 8, 8)
            n = ORDER[dst]
            if other is None:
                parts[n, at] = parts[n, at] + src[frm]
            else:
                total = parts[n, at].astype(F32) + src[frm].astype(F32) + other[frm].astype(F32)
                parts[n, at] = total.astype(BF16)

        loop(step, 0, count // 8)

    oz_cross = (
        rcopy(part(1, 3, hi), zq1.at[lo], zm),
        rcopy(part(2, 3, lo), zq2.at[lo], zp),
    )
    oy_half = {
        j: (
            rcopy(part(j, 3, lo), ya.at[n], ym),
            rcopy(part(j, 3, hi), yb.at[n], yp),
        )
        for n, j in enumerate((0, 3))
    }
    oy_side = (
        rcopy(part(1, 3, lo), ya.at[2], ym),
        rcopy(part(2, 3, hi), yb.at[2], yp),
    )
    oy_full = {
        j: (
            rcopy(part(j, 1), yf1.at[j], ym),
            rcopy(part(j, 2), yf2.at[j], yp),
        )
        for j in (0,)
    }
    oy_far = tuple(
        (
            rcopy(part(3, 1, blocks), yf1.at[3, blocks], ym),
            rcopy(part(3, 2, blocks), yf2.at[3, blocks], yp),
        )
        for blocks in (lo, hi)
    )
    oy_early = (
        rcopy(part(2, 1), yf1.at[2], ym),
        rcopy(part(1, 2), yf2.at[1], yp),
    )
    oy_next = (
        rcopy(part(1, 1, hi), yf1.at[1, hi], ym),
        rcopy(part(2, 2, lo), yf2.at[2, lo], yp),
    )
    oy_last = (
        rcopy(part(1, 1, lo), yf1.at[1, lo], ym),
        rcopy(part(2, 2, hi), yf2.at[2, hi], yp),
    )
    oz_half = (
        rcopy(part(3, 0, lo), za.at[lo], zm),
        rcopy(part(3, 0, hi), zb.at[lo], zp),
    )
    oz_first = (
        rcopy(part(1, 0, hi), zf1.at[hi], zm),
        rcopy(part(2, 0, lo), zf2.at[lo], zp),
    )
    oz_second = (
        rcopy(part(1, 0, lo), zf1.at[lo], zm),
        rcopy(part(2, 0, hi), zf2.at[hi], zp),
    )

    def y_end(j, first=0, count=DB):
        at = pl.ds(first, count)
        add_blocks((j, 0), yf1.at[j, at], first, count, yf2.at[j, at])

    start(oy_early)
    arrived(z_cross)
    y_far[0][1].wait_recv()
    y_far[1][0].wait_recv()
    arrived(y_relay_far)
    forward(2)
    spread(10, 6, 0, DB // 4)
    oy_half[3][0].start()
    oz_cross[1].start()
    spread(10, 6, DB // 4, DB // 2)
    oy_half[3][1].start()
    oz_cross[0].start()

    steps = (0, 3, 1, 2)
    base = len(copies)
    CORE, XH1, XH2, XF1, XF2, ZLO = (base + 8 * i for i in range(6))

    def core_copy(c):
        return make(wg.at[1, c], core_in.at[c], CORE + c, other_core)

    def x_half(c):
        return (
            make(wg.at[0, c, 6], xa.at[c], XH1 + c, xm),
            make(wg.at[0, c, 7], xb.at[c], XH2 + c, xp),
        )

    def x_full(c):
        return (
            make(wg.at[0, c, pl.ds(2, 2)], xf1.at[c], XF1 + c, xm),
            make(wg.at[0, c, pl.ds(4, 2)], xf2.at[c], XF2 + c, xp),
        )

    def z_low(c):
        return make(wg.at[0, c, 1], zr.at[c], ZLO + c, other_zl)

    def add_core(c):
        core_copy(c).wait_recv()
        for i in (6, 7, 2, 3, 4, 5, 0, 1):
            wg[0, c, i] = wg[0, c, i] + core_in[c, i]
        start(x_half(c))

    def add_x_half(c):
        arrived(x_half(c))
        wg[0, c, 2] = wg[0, c, 2] + xa[c]
        wg[0, c, 5] = wg[0, c, 5] + xb[c]
        start(x_full(c))

    def add_x_full(c):
        arrived(x_full(c))
        wg[0, c, 1] = (
            wg[0, c, 1].astype(F32) + xf1[c, 1].astype(F32) + xf2[c, 1].astype(F32)
        ).astype(BF16)
        z_low(c).start()

    def finish(c):
        z_low(c).wait_recv()
        total = (
            wg[0, c, 0].astype(F32) + xf1[c, 0].astype(F32) + xf2[c, 0].astype(F32)
            + zr[c].astype(F32)
        )
        igrad_ref[0, c] = total[:BLK].T
        ograd_ref[0, c] = total[BLK:]

    def weight_grad(c):
        left = gmat[c].T
        for rc in (1, 0):
            for rx in range(4):
                tiles, masks = [], []
                for rz in range(2):
                    k = (
                        lax.rem(x + steps[rx], 4) * 4
                        + lax.rem(zl + rz, 2) * 2
                        + lax.rem(core + rc, 2)
                    )
                    b = slot(k, c)
                    tiles.append(
                        jnp.concatenate(
                            [X[g][:, b].reshape(len(GROUPS[g]) * PAIR, BLK) for g in range(3)], axis=0
                        )
                    )
                    masks.append(mask(k, c) * grad_scale)
                res = jnp.dot(left, jnp.concatenate(tiles, axis=1), preferred_element_type=F32)
                for rz in range(2):
                    wg[rc, c, rx * 2 + rz] = (
                        res[:, rz * BLK : (rz + 1) * BLK] * masks[rz]
                    ).astype(BF16)
            if rc == 1:
                core_copy(c).start()

        @pl.when(c >= 1)
        def _():
            add_core(c - 1)

        @pl.when(c == 3)
        def _():
            oy_half[3][0].wait_recv()
            add_blocks((3, 1), ya.at[1], 0, HALF)
            oy_half[3][1].wait_recv()
            add_blocks((3, 2), yb.at[1], HALF, HALF)
            start(oy_far[0])

        @pl.when(c == 5)
        def _():
            start(oy_far[1])

        @pl.when(c == 7)
        def _():
            arrived(oy_far[0])
            y_end(3, 0, HALF)
            oz_half[0].start()

    loop(weight_grad, 0, COLS)
    add_core(COLS - 1)
    start(oy_next)
    arrived(oz_cross)
    add_blocks((0, 3), zq1, HALF, HALF)
    add_blocks((0, 3), zq2, 0, HALF)
    arrived(oy_far[1])
    y_end(3, HALF, HALF)
    oz_half[1].start()
    start(oy_side)
    loop(add_x_half, 0, 6)
    arrived(oy_early)
    arrived(oy_next)
    y_end(1, HALF, HALF)
    oz_first[0].start()
    y_end(2, 0, HALF)
    oz_first[1].start()
    loop(add_x_half, 6, COLS)
    loop(add_x_full, 0, 1)
    oy_side[0].wait_recv()
    add_blocks((1, 1), ya.at[2], 0, HALF)
    oy_last[0].start()
    oy_side[1].wait_recv()
    add_blocks((2, 2), yb.at[2], HALF, HALF)
    oy_last[1].start()
    start(oy_half[0])
    oz_half[0].wait_recv()
    add_blocks((1, 0), za, 0, HALF)
    oz_half[1].wait_recv()
    add_blocks((2, 0), zb, HALF, HALF)
    arrived(oy_last)
    y_end(1, 0, HALF)
    oz_second[0].start()
    y_end(2, HALF, HALF)
    oz_second[1].start()
    loop(add_x_full, 1, 4)
    oy_half[0][0].wait_recv()
    add_blocks((0, 1), ya.at[0], 0, HALF)
    oy_full[0][0].start()
    oy_half[0][1].wait_recv()
    add_blocks((0, 2), yb.at[0], HALF, HALF)
    oy_full[0][1].start()
    loop(add_x_full, 4, COLS)
    loop(finish, 0, 4)
    arrived(oy_full[0])
    y_end(0)
    loop(finish, 4, COLS)
    arrived(oz_first)
    arrived(oz_second)
    for b in range(DB):
        total = parts[0, b].astype(F32) + zf1[b].astype(F32) + zf2[b].astype(F32)
        cols = pl.ds(b * BLK, BLK)
        mixed_ref[:, cols] = total[:ROWS].astype(BF16)
        tgrad_ref[:, cols] = total[ROWS:].astype(BF16)

    for c in copies:
        c.wait_send()

    def sent(c):
        core_copy(c).wait_send()
        for r in (*x_half(c), *x_full(c)):
            r.wait_send()
        z_low(c).wait_send()

    loop(sent, 0, COLS)


def hand_on(*refs):
    n = len(refs) // 2
    for i in range(n):
        refs[n + i][...] = refs[i][...]


def body(tokens, cotangent, w_in, w_out, block_index, live_count):
    grad_scale = 1.0 / math.sqrt(tokens.shape[0] * lax.axis_size("hid") * lax.axis_size("dp"))
    vmem = pl.BlockSpec(memory_space=pltpu.VMEM)
    smem = pl.BlockSpec(memory_space=pltpu.SMEM)
    hbm = pl.BlockSpec(memory_space=pl.ANY)
    half = (HALF, PAIR, BLK)
    full = (DB, PAIR, BLK)
    tile = (2 * BLK, BLK)
    shapes = (
        jax.ShapeDtypeStruct(tokens.shape, BF16),
        jax.ShapeDtypeStruct(tokens.shape, BF16),
        jax.ShapeDtypeStruct((1, COLS, BLK, BLK), F32),
        jax.ShapeDtypeStruct((1, COLS, BLK, BLK), F32),
    )
    results = pl.pallas_call(
        functools.partial(kernel, grad_scale),
        out_shape=shapes,
        in_specs=[smem, smem, vmem, vmem, hbm, hbm],
        out_specs=(vmem, vmem, vmem, vmem),
        scratch_shapes=[
            *[pltpu.VMEM((len(g), *full), BF16) for g in GROUPS],
            pltpu.VMEM((16, *full), BF16),
            pltpu.VMEM((COLS, SLOTS * BLK, 2 * BLK), BF16),
            pltpu.VMEM((SLOTS + 1, COLS, BLK, BLK), BF16),
            pltpu.VMEM((SLOTS + 1, COLS, BLK, BLK), BF16),
            pltpu.VMEM((COLS, 16 * ROWS, BLK), BF16),
            pltpu.VMEM((COLS, 16 * ROWS, BLK), BF16),
            pltpu.VMEM((COLS, 16 * PAIR, 2 * BLK), BF16),
            pltpu.VMEM((2, COLS, 8, *tile), BF16),
            pltpu.VMEM((COLS, 8, *tile), BF16),
            pltpu.VMEM((COLS, *tile), BF16),
            pltpu.VMEM((COLS, *tile), BF16),
            pltpu.VMEM((COLS, 2, *tile), BF16),
            pltpu.VMEM((COLS, 2, *tile), BF16),
            pltpu.VMEM((COLS, *tile), BF16),
            pltpu.VMEM((3, *half), BF16),
            pltpu.VMEM((3, *half), BF16),
            pltpu.VMEM((4, *full), BF16),
            pltpu.VMEM((4, *full), BF16),
            pltpu.VMEM(half, BF16),
            pltpu.VMEM(half, BF16),
            *[pltpu.VMEM(full, BF16) for _ in range(2)],
            *[pltpu.VMEM(half, BF16) for _ in range(2)],
            pltpu.SMEM((COLS, DB), jnp.int32),
            pltpu.SemaphoreType.DMA((2 * SLOTS,)),
            pltpu.SemaphoreType.DMA((COPIES,)),
            pltpu.SemaphoreType.DMA((COPIES,)),
        ],
        compiler_params=pltpu.CompilerParams(
            collective_id=0, has_side_effects=True, vmem_limit_bytes=62 * 2**20
        ),
        cost_estimate=pl.CostEstimate(
            flops=3 * 2 * 2 * 384 * 2048 * 1024, bytes_accessed=12 * 2**20, transcendentals=384 * 1024
        ),
    )(block_index.T, live_count, tokens, cotangent, w_in, w_out)
    return pl.pallas_call(
        hand_on,
        out_shape=shapes,
        in_specs=[vmem] * len(shapes),
        out_specs=(vmem,) * len(shapes),
    )(*results)


def solution(mesh):
    in_specs = (
        P(("dp", "hid"), None),
        P(("dp", "hid"), None),
        P(None, "hid", None, None),
        P(None, "hid", None, None),
        P(None, "hid"),
        P("hid"),
    )
    out_specs = (
        P(("dp", "hid"), None),
        P(("dp", "hid"), None),
        P("dp", "hid", None, None),
        P("dp", "hid", None, None),
    )
    return jax.shard_map(body, mesh=mesh, in_specs=in_specs, out_specs=out_specs, check_vma=False)
```
